256 devices in a mesh: row: 8 (over x, core), col: 32 (over z, y).
Axes of the slice: x: 4, y: 4, z: 8, core: 2. Of those that a mesh axis runs over, the one named last changes fastest.
Arguments:
- inputs: bfloat16 [1024, 8192], P('col', 'row'), may hold values from -6 to 6
- cotangent: bfloat16 [1024, 8192], P('col', 'row'), may hold values from -6 to 6
- gate_pre: bfloat16 [1024, 28672], P('row', 'col'), may hold values from -6 to 6
- up_pre: bfloat16 [1024, 28672], P('row', 'col'), may hold values from -6 to 6
- gate_weight: bfloat16 [8192, 28672], P('row', 'col'), may hold values from -0.0625 to 0.0625
- up_weight: bfloat16 [8192, 28672], P('row', 'col'), may hold values from -0.0625 to 0.0625
- down_weight: bfloat16 [28672, 8192], P('col', 'row'), may hold values from -0.03125 to 0.03125
- pair_ids: int32 [1024], P('col'), may hold values from 0 to 7, never falling along the last dimension, each value on 1 to 512 neighbouring positions
- flags: int32 [1024], P('col'), may hold values 0 or 1
- pair_scale: float32 [8], replicated, may hold values from 0.5 to 2
Outputs:
- grad_input: bfloat16 [1024, 8192], P('col', 'row')
- grad_gate: bfloat16 [8192, 28672], P('row', 'col')
- grad_up: bfloat16 [8192, 28672], P('row', 'col')
- grad_down: bfloat16 [28672, 8192], P('col', 'row')
The draws below stay inside these ranges and needn't reach their ends.
Inputs may be any that keep to these rules, and one draw needn't show every extreme that they name: `pair_ids`: never falls from one token to the next.
All inputs are finite; a program needn't handle non-finite values. No bound on the sum of `flags` on one device may be relied on, other than what follows from the above.
Results may differ from the reference program's by a relative error of at most 0.0057.
Values may be sent and summed in bfloat16 or wider, within the bound.
No kernel may reach another device: no remote copies, remote signals or barrier semaphores. Data moves between devices by JAX's collectives and lax.ppermute only.
A program may use at most 128 MiB of HBM per device.

```python
import math
import jax
import jax.numpy as jnp
import numpy as np

D = 8192
FF = 28672
PAIRS = 8
TOKENS = 1024


def plant(array, rng, smallest, high):
    index_at = [jax.random.randint(jax.random.fold_in(rng, axis), (), 0, length) for axis, length in enumerate(array.shape)]
    main_axis = array.shape.index(max(array.shape))
    next_to = index_at[:main_axis] + [(index_at[main_axis] + 1) % array.shape[main_axis]] + index_at[main_axis + 1:]
    return array.at[tuple(index_at)].set(smallest).at[tuple(next_to)].set(high)


def steps_of(own_key, dims, pieces, smallest, high):
    level, own = 1.0, jax.random.fold_in(own_key, 6)
    for position, shards_of in pieces:
        steps = jnp.exp(jax.random.uniform(jax.random.fold_in(own, position), (shards_of,), jnp.float32, smallest / len(pieces), high / len(pieces)))
        level = level * jnp.repeat(steps, dims[position] // shards_of).reshape([-1 if axis == position else 1 for axis in range(len(dims))])
    return level


def profile(amount, total, most, slope):
    weights = [(1 << 20) // math.isqrt(standing ** slope) + 1 for standing in range(2, amount + 1)]
    rest, counts = total - most - (amount - 1), [1] * (amount - 1)
    while rest > 0:
        free = [i for i in range(amount - 1) if counts[i] < most]
        pool, remaining = sum([weights[i] for i in free]), rest
        for i in free:
            addition = min(most - counts[i], max(1, remaining * weights[i] // pool), rest)
            counts[i] = counts[i] + addition
            rest = rest - addition
    return np.array([most] + counts)


def uneven(stream_key, amount, total, limit, skew):
    if amount == 2:
        one = jax.random.randint(stream_key, (), max(1, total - limit), min(limit, total - 1) + 1)
        return jnp.stack([one, total - one])
    sizes = jnp.asarray(profile(amount, total, limit, skew), jnp.int32)
    twos = (amount - 1) // 2
    source_of, sink = sizes[1:1 + 2 * twos:2], sizes[2:2 + 2 * twos:2]
    room = jnp.minimum(source_of - 1, limit - sink)
    passed = jax.random.randint(jax.random.fold_in(stream_key, 1), (twos,), 0, 1 << 20) % (room + 1)
    sizes = sizes.at[1:1 + 2 * twos:2].set(source_of - passed).at[2:2 + 2 * twos:2].set(sink + passed)
    return sizes[jax.random.permutation(jax.random.fold_in(stream_key, 2), amount)]


def normal_values(stream_key, extent, width, most, split=(), kind=jnp.bfloat16):
    level = steps_of(stream_key, extent, split, -0.22, 0.18) if split else 1.0
    array = jax.random.normal(stream_key, extent, jnp.float32) * width * level
    return jnp.minimum(jnp.maximum(array, -most), most).astype(kind)


def setup_inputs(seed: int = 0) -> dict:
    seeds = jax.random.split(jax.random.key(seed), 11)
    return {
        "inputs": normal_values(seeds[0], (TOKENS, D), 1.0, 6.0, ((0, 32), (1, 8))),
        "cotangent": normal_values(seeds[1], (TOKENS, D), 1.0, 6.0, ((0, 32), (1, 8))),
        "gate_pre": normal_values(seeds[2], (TOKENS, FF), 1.0, 6.0, ((0, 8), (1, 32))),
        "up_pre": normal_values(seeds[3], (TOKENS, FF), 1.0, 6.0, ((0, 8), (1, 32))),
        "gate_weight": normal_values(seeds[4], (D, FF), D ** -0.5, 0.0625, ((0, 8), (1, 32))),
        "up_weight": normal_values(seeds[5], (D, FF), D ** -0.5, 0.0625, ((0, 8), (1, 32))),
        "down_weight": normal_values(seeds[6], (FF, D), FF ** -0.5, 0.03125, ((0, 32), (1, 8))),
        "pair_ids": jnp.searchsorted(jnp.cumsum(uneven(seeds[7], PAIRS, TOKENS, TOKENS // 2, 0)), jnp.arange(TOKENS), side="right").astype(jnp.int32),
        "flags": plant((jax.random.randint(seeds[8], (TOKENS,), 0, 2) < 1).astype(jnp.int32), jax.random.fold_in(seeds[8], 1), 0, 1),
        "pair_scale": jnp.clip(jnp.exp(jax.random.uniform(seeds[9], (PAIRS,), jnp.float32, math.log(0.5), math.log(2.0))), 0.5, 2.0),
    }


def reference(inputs, cotangent, gate_pre, up_pre, gate_weight, up_weight, down_weight, pair_ids, flags, pair_scale):
    matches = pair_ids[:, None] == jnp.arange(PAIRS, dtype=jnp.int32)[None, :]
    scales = jnp.sum(jnp.where(matches, pair_scale[None, :], jnp.zeros((), pair_scale.dtype)), axis=1)
    weight = (2 * flags - 1).astype(jnp.float32) * scales.astype(jnp.float32)
    scaled = (cotangent.astype(jnp.float32) * weight[:, None]).astype(jnp.bfloat16)
    d_hidden = jnp.dot(scaled, down_weight.T, preferred_element_type=jnp.float32)
    gate_f = gate_pre.astype(jnp.float32)
    up_f = up_pre.astype(jnp.float32)
    sigmoid_gate = jax.nn.sigmoid(gate_f)
    hidden = (gate_f * sigmoid_gate * up_f).astype(jnp.bfloat16)
    d_up = (d_hidden * gate_f * sigmoid_gate).astype(jnp.bfloat16)
    d_gate = (d_hidden * up_f * sigmoid_gate * (1.0 + gate_f * (1.0 - sigmoid_gate))).astype(jnp.bfloat16)
    grad_down = jnp.dot(hidden.T, scaled, preferred_element_type=jnp.float32).astype(jnp.bfloat16)
    grad_gate = jnp.dot(inputs.T, d_gate, preferred_element_type=jnp.float32).astype(jnp.bfloat16)
    grad_up = jnp.dot(inputs.T, d_up, preferred_element_type=jnp.float32).astype(jnp.bfloat16)
    grad_input = (jnp.dot(d_gate, gate_weight.T, preferred_element_type=jnp.float32)
                  + jnp.dot(d_up, up_weight.T, preferred_element_type=jnp.float32)).astype(jnp.bfloat16)
    return grad_input, grad_gate, grad_up, grad_down
```

```python
import jax
import jax.numpy as jnp
from jax import lax
from jax.experimental import pallas as pl
from jax.experimental.pallas import tpu as pltpu
from jax.sharding import PartitionSpec as P

NX, NC, NZ, NY = 4, 2, 8, 4
TOK = 32
BLK = NY * TOK
BF, F32 = jnp.bfloat16, jnp.float32


def from_z(v, k):
    perm = [(z * NY + y, (z - k) % NZ * NY + y) for z in range(NZ) for y in range(NY)]
    return lax.ppermute(v, "col", perm)


def from_y(v, k):
    perm = [(z * NY + y, z * NY + (y - k) % NY) for z in range(NZ) for y in range(NY)]
    return lax.ppermute(v, "col", perm)


def from_x(v, k):
    perm = [(x * NC + c, (x - k) % NX * NC + c) for x in range(NX) for c in range(NC)]
    return lax.ppermute(v, "row", perm)


def from_core(v):
    return lax.ppermute(v, "row", [(r, r ^ 1) for r in range(NX * NC)])


def halves_kernel(u, d, r1, r2, r3, low, high):
    half = BLK // 2
    low[...] = u[:half, :]
    high[...] = d[half:, :]


def halves(u, d, after):
    block = pl.BlockSpec(u.shape, lambda t: (0, 0))
    half = pl.BlockSpec((BLK // 2, u.shape[1]), lambda t: (0, 0))
    sds = jax.ShapeDtypeStruct((BLK // 2, u.shape[1]), BF)
    return pl.pallas_call(
        halves_kernel,
        grid=(1,),
        in_specs=[block, block] + [pl.BlockSpec(memory_space=pl.ANY)] * 3,
        out_specs=[half, half],
        out_shape=[sds, sds],
        compiler_params=pltpu.CompilerParams(vmem_limit_bytes=4 << 20),
        cost_estimate=pl.CostEstimate(flops=0, bytes_accessed=4 * u.size, transcendentals=0),
        name="halves",
    )(u, d, *after)


def gather_z(blk, pre_of):
    up, down = [blk], [blk]
    for r in range(3):
        up.append(from_z(up[-1], 1))
        down.append(from_z(down[-1], -1))
        if r == 0:
            pre = pre_of(up[-1])
            others = [from_x(pre, k) for k in range(1, NX)]
    low, high = halves(up[3], down[3], others)
    far = [from_z(low, 1), from_z(high, -1)]
    all_rows = jnp.concatenate(up + far + [down[3], down[2], down[1]], axis=0)
    return all_rows, jnp.stack([pre] + others, axis=0)


def near_kernel(b3, b5, up, down, after, up_out, down_out):
    half = BLK // 2
    up_out[:half, :] = (b3[:half, :].astype(F32) + up[...].astype(F32)).astype(BF)
    up_out[half:, :] = b3[half:, :]
    down_out[:half, :] = b5[:half, :]
    down_out[half:, :] = (b5[half:, :].astype(F32) + down[...].astype(F32)).astype(BF)


def step_kernel(bu, bd, up, down, after, up_out, down_out):
    up_out[...] = (bu[...].astype(F32) + up[...].astype(F32)).astype(BF)
    down_out[...] = (bd[...].astype(F32) + down[...].astype(F32)).astype(BF)


def step(kernel, p, i, j, up, down, after):
    width = p.shape[1]
    sds = jax.ShapeDtypeStruct((BLK, width), BF)
    whole = pl.BlockSpec(up.shape, lambda t: (0, 0))
    block = pl.BlockSpec((BLK, width), lambda t: (0, 0))
    return pl.pallas_call(
        kernel,
        grid=(1,),
        in_specs=[
            pl.BlockSpec((BLK, width), lambda t: (i, 0)),
            pl.BlockSpec((BLK, width), lambda t: (j, 0)),
            whole,
            whole,
            pl.BlockSpec(memory_space=pl.ANY),
        ],
        out_specs=[block, block],
        out_shape=[sds, sds],
        compiler_params=pltpu.CompilerParams(vmem_limit_bytes=6 << 20),
        cost_estimate=pl.CostEstimate(flops=2 * BLK * width, bytes_accessed=12 * BLK * width, transcendentals=0),
        name="step",
    )(p, p, up, down, after)


def own_kernel(b0, up, down, after, own, s1, s2, s3):
    total = b0[...].astype(F32) + up[...].astype(F32) + down[...].astype(F32)
    own[...] = total[:TOK, :]
    for k, out in enumerate((s1, s2, s3), 1):
        out[...] = total[k * TOK:(k + 1) * TOK, :].astype(BF)


def own_of(p, up, down, after):
    width = p.shape[1]
    block = pl.BlockSpec((BLK, width), lambda t: (0, 0))
    out = pl.BlockSpec((TOK, width), lambda t: (0, 0))
    return pl.pallas_call(
        own_kernel,
        grid=(1,),
        in_specs=[block] * 3 + [pl.BlockSpec(memory_space=pl.ANY)],
        out_specs=[out] * 4,
        out_shape=[jax.ShapeDtypeStruct((TOK, width), F32)] + [jax.ShapeDtypeStruct((TOK, width), BF)] * 3,
        compiler_params=pltpu.CompilerParams(vmem_limit_bytes=6 << 20),
        cost_estimate=pl.CostEstimate(flops=2 * BLK * width, bytes_accessed=8 * BLK * width, transcendentals=0),
        name="own",
    )(p, up, down, after)


def scatter_z_y(p, marks):
    half = BLK // 2
    far = p[4 * BLK:5 * BLK]
    up, down = from_z(far[:half], -1), from_z(far[half:], 1)
    up, down = step(near_kernel, p, 3, 5, up, down, marks[0])
    for n, i, j in ((1, 2, 6), (2, 1, 7)):
        up, down = step(step_kernel, p, i, j, from_z(up, -1), from_z(down, 1), marks[n])
    own, *sent = own_of(p, from_z(up, -1), from_z(down, 1), marks[3])
    return total_of(own, [from_y(v, -k) for k, v in enumerate(sent, 1)], own)


def weigh_kernel(ids, flags, scale, cot, x, out):
    row = lax.broadcasted_iota(jnp.int32, cot.shape, 0)
    weight = jnp.zeros(cot.shape, F32)
    for r in range(TOK):
        w = (2 * flags[r] - 1).astype(F32) * scale[ids[r]]
        weight = jnp.where(row == r, w, weight)
    out[:TOK, :] = (cot[...].astype(F32) * weight).astype(BF)
    out[TOK:, :] = x[...]


def weigh(cotangent, inputs, pair_ids, flags, pair_scale):
    smem = pl.BlockSpec(memory_space=pltpu.SMEM)
    vmem = pl.BlockSpec(memory_space=pltpu.VMEM)
    return pl.pallas_call(
        weigh_kernel,
        in_specs=[smem, smem, smem, vmem, vmem],
        out_specs=vmem,
        out_shape=jax.ShapeDtypeStruct((2 * TOK, cotangent.shape[1]), BF),
        compiler_params=pltpu.CompilerParams(vmem_limit_bytes=60 << 20),
        cost_estimate=pl.CostEstimate(flops=cotangent.size, bytes_accessed=4 * cotangent.size, transcendentals=0),
        name="weigh",
    )(pair_ids, flags, pair_scale, cotangent, inputs)


def prep_kernel(s, mine, other, after, hidden_t, a_out, b_out, mark):
    y = s[3]
    same = lax.rem(lax.rem(s[2] + pl.program_id(0), NZ), NC) == s[1]

    def turned(i):
        rows = [pl.ds(pl.multiple_of(lax.rem(y + j, NY) * TOK, TOK), TOK) for j in range(NY)]
        got = [jnp.where(same, mine[0, i, r, :], other[0, i, r, :]) for r in rows]
        return jnp.concatenate(got, axis=0).astype(F32)

    g, u = turned(0), turned(1)
    sig = 1.0 / (1.0 + jnp.exp(-g))
    gs = g * sig
    a_out[...] = gs
    b_out[...] = u * sig * (1.0 + g * (1.0 - sig))
    hidden_t[...] = (gs * u).astype(BF).T
    mark[...] = jnp.zeros(mark.shape, F32)


def prep(place, mine, other, after):
    ff = mine.shape[-1]
    tokens = NZ * BLK

    def piece(t, s):
        block = lax.rem(s[2] + t, NZ)
        return (lax.rem(lax.div(block, NC) - s[0] + NX, NX), 0, 0, 0)

    spec = pl.BlockSpec((1, 2, BLK, ff), piece)
    return pl.pallas_call(
        prep_kernel,
        grid_spec=pltpu.PrefetchScalarGridSpec(
            num_scalar_prefetch=1,
            grid=(NZ,),
            in_specs=[
                spec,
                spec,
                pl.BlockSpec(memory_space=pl.ANY),
            ],
            out_specs=[
                pl.BlockSpec((ff, BLK), lambda t, s: (0, t)),
                pl.BlockSpec((BLK, ff), lambda t, s: (t, 0)),
                pl.BlockSpec((BLK, ff), lambda t, s: (t, 0)),
                pl.BlockSpec((8, 128), lambda t, s: (0, 0)),
            ],
        ),
        out_shape=[
            jax.ShapeDtypeStruct((ff, tokens), BF),
            jax.ShapeDtypeStruct((tokens, ff), F32),
            jax.ShapeDtypeStruct((tokens, ff), F32),
            jax.ShapeDtypeStruct((8, 128), F32),
        ],
        compiler_params=pltpu.CompilerParams(vmem_limit_bytes=8 << 20),
        cost_estimate=pl.CostEstimate(flops=30 * tokens * ff, bytes_accessed=14 * tokens * ff, transcendentals=0),
        name="prep",
    )(place, mine, other, after)


def turn_kernel(s, x_in, after, x_out, mark):
    x_out[...] = x_in[...].T
    mark[...] = jnp.zeros(mark.shape, F32)


def turn(place, x_all, after):
    tokens, width = x_all.shape
    return pl.pallas_call(
        turn_kernel,
        grid_spec=pltpu.PrefetchScalarGridSpec(
            num_scalar_prefetch=1,
            grid=(NZ,),
            in_specs=[
                pl.BlockSpec((BLK, width), lambda t, s: (lax.rem(s[2] + t, NZ), 0)),
                pl.BlockSpec(memory_space=pl.ANY),
            ],
            out_specs=[
                pl.BlockSpec((width, BLK), lambda t, s: (0, t)),
                pl.BlockSpec((8, 128), lambda t, s: (0, 0)),
            ],
        ),
        out_shape=[jax.ShapeDtypeStruct((width, tokens), BF), jax.ShapeDtypeStruct((8, 128), F32)],
        compiler_params=pltpu.CompilerParams(vmem_limit_bytes=8 << 20),
        cost_estimate=pl.CostEstimate(flops=0, bytes_accessed=4 * tokens * width, transcendentals=0),
        name="turn",
    )(place, x_all, after)


def nt(a, b):
    return lax.dot_general(a, b, (((1,), (1,)), ((), ())), preferred_element_type=F32)


def first_kernel(s, dy, w, out):
    x = s[0]
    for b in range(2):
        acc = nt(dy[b * 256:(b + 1) * 256, :], w[...]).astype(out.dtype)
        for h in range(2):
            t = 2 * b + h
            at = pl.multiple_of(lax.rem(t - x + NX, NX) * BLK, BLK)
            out[pl.ds(at, BLK), :] = acc[h * BLK:(h + 1) * BLK, :]


def first(place, dy_all, down_weight, flip, dtype):
    tokens, width = dy_all.shape
    ff = down_weight.shape[0]
    half = tokens // 2
    return pl.pallas_call(
        first_kernel,
        grid_spec=pltpu.PrefetchScalarGridSpec(
            num_scalar_prefetch=1,
            grid=(1,),
            in_specs=[
                pl.BlockSpec((half, width), lambda i, s: (lax.rem(s[1] + flip, NC), 0)),
                pl.BlockSpec((ff, width), lambda i, s: (0, 0)),
            ],
            out_specs=pl.BlockSpec((half, ff), lambda i, s: (0, 0)),
        ),
        out_shape=jax.ShapeDtypeStruct((half, ff), dtype),
        compiler_params=pltpu.CompilerParams(vmem_limit_bytes=14 << 20),
        cost_estimate=pl.CostEstimate(flops=2 * half * ff * width, bytes_accessed=2 * (half * width + ff * width + half * ff), transcendentals=0),
        name="first",
    )(place, dy_all, down_weight)


def second_kernel(s, m0, m1, o0, o1, a, b, gw, uw, dg, du, p):
    x, c = s[0], s[1]
    half = lax.div(pl.program_id(0), 2)
    same = half == c
    for h, (m, o) in enumerate(((m0, o0), (m1, o1))):
        rows = pl.ds(h * BLK, BLK)
        d = jnp.where(same, m[...], o[...]).astype(F32)
        du[rows, :] = (d * a[rows, :]).astype(BF)
        dg[rows, :] = (d * b[rows, :]).astype(BF)
    p[...] = (nt(dg[...], gw[...]) + nt(du[...], uw[...])).astype(BF)


def second(place, mine, other, a, b, gate_weight, up_weight):
    tokens, ff = a.shape
    width = gate_weight.shape[0]

    def at(h):
        return pl.BlockSpec(
            (BLK, ff), lambda t, s: (lax.rem(lax.rem(2 * t + h, NX) - s[0] + NX, NX), 0)
        )

    tile = 2 * BLK
    row = pl.BlockSpec((tile, ff), lambda t, s: (t, 0))
    whole = pl.BlockSpec((width, ff), lambda t, s: (0, 0))
    return pl.pallas_call(
        second_kernel,
        grid_spec=pltpu.PrefetchScalarGridSpec(
            num_scalar_prefetch=1,
            grid=(tokens // tile,),
            in_specs=[at(0), at(1), at(0), at(1), row, row, whole, whole],
            out_specs=[row, row, pl.BlockSpec((tile, width), lambda t, s: (t, 0))],
        ),
        out_shape=[
            jax.ShapeDtypeStruct((tokens, ff), BF),
            jax.ShapeDtypeStruct((tokens, ff), BF),
            jax.ShapeDtypeStruct((tokens, width), BF),
        ],
        compiler_params=pltpu.CompilerParams(vmem_limit_bytes=22 << 20),
        cost_estimate=pl.CostEstimate(flops=4 * tokens * ff * width, bytes_accessed=2 * (8 * tokens * ff + 2 * ff * width), transcendentals=0),
        name="second",
    )(place, mine, mine, other, other, a, b, gate_weight, up_weight)


def pack_kernel(g, u, after, out):
    out[0] = g[...]
    out[1] = u[...]


def pack(gate_pre, up_pre, after):
    vmem = pl.BlockSpec(memory_space=pltpu.VMEM)
    return pl.pallas_call(
        pack_kernel,
        in_specs=[vmem, vmem, pl.BlockSpec(memory_space=pl.ANY)],
        out_specs=vmem,
        out_shape=jax.ShapeDtypeStruct((2,) + gate_pre.shape, BF),
        compiler_params=pltpu.CompilerParams(vmem_limit_bytes=60 << 20),
        cost_estimate=pl.CostEstimate(flops=0, bytes_accessed=8 * gate_pre.size, transcendentals=0),
        name="pack",
    )(gate_pre, up_pre, after)


def total_kernel(own, r1, r2, r3, after, out):
    out[...] = (own[...] + r1[...].astype(F32) + r2[...].astype(F32) + r3[...].astype(F32)).astype(BF)


def total_of(own, parts, after):
    vmem = pl.BlockSpec(memory_space=pltpu.VMEM)
    return pl.pallas_call(
        total_kernel,
        in_specs=[vmem] * 4 + [pl.BlockSpec(memory_space=pl.ANY)],
        out_specs=vmem,
        out_shape=jax.ShapeDtypeStruct(own.shape, BF),
        compiler_params=pltpu.CompilerParams(vmem_limit_bytes=8 << 20),
        cost_estimate=pl.CostEstimate(flops=3 * own.size, bytes_accessed=12 * own.size, transcendentals=0),
        name="total",
    )(own, *parts, after)


def product_kernel(a, b, after, out, mark):
    out[...] = jnp.dot(a[...], b[...], preferred_element_type=F32).astype(BF)
    mark[...] = jnp.zeros(mark.shape, F32)


def product(a, b, tile, after):
    m, k = a.shape
    n = b.shape[1]
    return pl.pallas_call(
        product_kernel,
        grid=(m // tile,),
        in_specs=[
            pl.BlockSpec((tile, k), lambda i: (i, 0)),
            pl.BlockSpec((k, n), lambda i: (0, 0)),
            pl.BlockSpec(memory_space=pl.ANY),
        ],
        out_specs=[pl.BlockSpec((tile, n), lambda i: (i, 0)), pl.BlockSpec((8, 128), lambda i: (0, 0))],
        out_shape=[jax.ShapeDtypeStruct((m, n), BF), jax.ShapeDtypeStruct((8, 128), F32)],
        compiler_params=pltpu.CompilerParams(vmem_limit_bytes=14 << 20),
        cost_estimate=pl.CostEstimate(flops=2 * m * k * n, bytes_accessed=2 * (m * k + k * n + m * n), transcendentals=0),
        name="product",
    )(a, b, after)


def on_device(
    inputs,
    cotangent,
    gate_pre,
    up_pre,
    gate_weight,
    up_weight,
    down_weight,
    pair_ids,
    flags,
    pair_scale,
):
    row, col = lax.axis_index("row"), lax.axis_index("col")
    place = jnp.stack([row // NC, row % NC, col // NY, col % NY]).astype(jnp.int32)
    both = weigh(cotangent, inputs, pair_ids, flags, pair_scale)
    rows = [both] + [from_y(both, k) for k in range(1, NY)]
    x_all = lax.all_gather(
        jnp.concatenate([v[TOK:] for v in rows], axis=0),
        "col",
        axis=0,
        tiled=True,
        axis_index_groups=[[z * NY + y for z in range(NZ)] for y in range(NY)],
    )
    dy_all, pre_mine = gather_z(
        jnp.concatenate([v[:TOK] for v in rows], axis=0),
        lambda v: pack(gate_pre, up_pre, v),
    )
    pre_other = from_core(pre_mine)

    sent = first(place, dy_all, down_weight, 1, BF)
    theirs = from_core(sent)
    hidden_t, a, b, ready = prep(place, pre_mine, pre_other, x_all[:16, :128])
    pair = first(place, dy_all, down_weight, 0, F32) + theirs.astype(F32)
    pair = pair.reshape(NX, BLK, -1)
    total = total_of(pair[0], [from_x(pair[k].astype(BF), -k) for k in range(1, NX)], ready)
    mine = jnp.concatenate([total] + [from_x(total, k) for k in range(1, NX)], axis=0)
    other = from_core(mine)
    d_gate, d_up, part = second(place, mine, other, a, b, gate_weight, up_weight)
    grad_down, mark_0 = product(hidden_t, dy_all, 448, part[:8, :128])
    x_t, mark_1 = turn(place, x_all, mark_0)
    grad_gate, mark_2 = product(x_t, d_gate, 512, mark_1)
    grad_up, mark_3 = product(x_t, d_up, 512, mark_2)
    grad_input = scatter_z_y(part, (mark_0, mark_1, mark_2, mark_3))
    return (grad_input, grad_gate, grad_up, grad_down)


def solution(mesh):
    return jax.shard_map(
        on_device,
        mesh=mesh,
        in_specs=(
            P("col", "row"),
            P("col", "row"),
            P("row", "col"),
            P("row", "col"),
            P("row", "col"),
            P("row", "col"),
            P("col", "row"),
            P("col"),
            P("col"),
            P(),
        ),
        out_specs=(P("col", "row"), P("row", "col"), P("row", "col"), P("col", "row")),
        check_vma=False,
    )
```

```python
import functools

import jax
import jax.numpy as jnp
from jax import lax
from jax.experimental import pallas as pl
from jax.experimental.pallas import tpu as pltpu
from jax.sharding import PartitionSpec as P

NX, NC, NZ, NY = 4, 2, 8, 4
TOK = 32
BLK = NY * TOK
HALF = BLK // NC
SUB = HALF // NX
ORDER = (0, 1, 2, 3, 5, 6, 7, 4)
BF, F32 = jnp.bfloat16, jnp.float32
HBM = pl.BlockSpec(memory_space=pltpu.HBM)
VMEM = pl.BlockSpec(memory_space=pltpu.VMEM)
SMEM = pl.BlockSpec(memory_space=pltpu.SMEM)


def stay(v):
    return pltpu.with_memory_space_constraint(v, pltpu.HBM)


def params(mib):
    return pltpu.CompilerParams(vmem_limit_bytes=mib << 20)


def cost(flops, size):
    return pl.CostEstimate(flops=flops, bytes_accessed=size, transcendentals=0)


def from_z(v, k):
    perm = [(z * NY + y, (z - k) % NZ * NY + y) for z in range(NZ) for y in range(NY)]
    return lax.ppermute(v, "col", perm)


def from_y(v, k):
    perm = [(z * NY + y, z * NY + (y - k) % NY) for z in range(NZ) for y in range(NY)]
    return lax.ppermute(v, "col", perm)


def from_x(v, k):
    perm = [(x * NC + c, (x - k) % NX * NC + c) for x in range(NX) for c in range(NC)]
    return lax.ppermute(v, "row", perm)


def from_core(v):
    return lax.ppermute(v, "row", [(r, r ^ 1) for r in range(NX * NC)])


def weigh_kernel(ids_in, flags_in, scale_in, cot_in, out, ids, flags, scale, cot, sems):
    copies = [
        pltpu.make_async_copy(src, dst, sems.at[i])
        for i, (src, dst) in enumerate(
            ((ids_in, ids), (flags_in, flags), (scale_in, scale), (cot_in, cot))
        )
    ]
    for copy in copies:
        copy.start()
    for copy in copies:
        copy.wait()
    row = lax.broadcasted_iota(jnp.int32, cot.shape, 0)
    weight = jnp.zeros(cot.shape, F32)
    for r in range(TOK):
        w = (2 * flags[r] - 1).astype(F32) * scale[ids[r]]
        weight = jnp.where(row == r, w, weight)
    out[...] = (cot[...].astype(F32) * weight).astype(BF)


def weigh(cotangent, pair_ids, flags, pair_scale):
    return pl.pallas_call(
        weigh_kernel,
        in_specs=[HBM] * 4,
        out_specs=VMEM,
        out_shape=jax.ShapeDtypeStruct(cotangent.shape, BF),
        scratch_shapes=[
            pltpu.SMEM(pair_ids.shape, jnp.int32),
            pltpu.SMEM(flags.shape, jnp.int32),
            pltpu.SMEM(pair_scale.shape, F32),
            pltpu.VMEM(cotangent.shape, BF),
            pltpu.SemaphoreType.DMA((4,)),
        ],
        compiler_params=params(4),
        cost_estimate=cost(cotangent.size, 8 * cotangent.size),
        name="weigh",
    )(*map(stay, (pair_ids, flags, pair_scale, cotangent)))


def lead_kernel(r0, r1, r2, r3, g, u, rows, pre, sems):
    copies = [pltpu.make_async_copy(v, pre.at[i], sems.at[i]) for i, v in enumerate((g, u))]
    for copy in copies:
        copy.start()
    for k, r in enumerate((r0, r1, r2, r3)):
        rows[k * TOK:(k + 1) * TOK, :] = r[...]
    for copy in copies:
        copy.wait()


def lead(parts, gate_pre, up_pre):
    return pl.pallas_call(
        lead_kernel,
        in_specs=[VMEM] * 4 + [HBM] * 2,
        out_specs=[VMEM, HBM],
        out_shape=[
            jax.ShapeDtypeStruct((BLK, parts[0].shape[1]), BF),
            pltpu.HBM((2,) + gate_pre.shape, BF),
        ],
        scratch_shapes=[pltpu.SemaphoreType.DMA((2,))],
        compiler_params=params(4),
        cost_estimate=cost(0, 8 * (parts[0].size * 2 + gate_pre.size)),
        name="lead",
    )(*parts, stay(gate_pre), stay(up_pre))


def halves_kernel(u, d, r1, r2, r3, low, high):
    low[...] = u[:HALF, :]
    high[...] = d[HALF:, :]


def halves(u, d, after):
    half = jax.ShapeDtypeStruct((HALF, u.shape[1]), BF)
    return pl.pallas_call(
        halves_kernel,
        in_specs=[VMEM] * 2 + [HBM] * 3,
        out_specs=[VMEM] * 2,
        out_shape=[half, half],
        compiler_params=params(4),
        cost_estimate=cost(0, 4 * u.size),
        name="halves",
    )(u, d, *after)


def nt(a, b):
    return lax.dot_general(a, b, (((1,), (1,)), ((), ())), preferred_element_type=F32)


def first_kernel(flip, s, dy, low, high, w, out):
    n = dy.shape[0]
    far = jnp.where(lax.rem(s[1] + flip, NC) == 0, low[...], high[...])
    rows = jnp.concatenate([dy[j] for j in range(n)] + [far], axis=0)
    acc = nt(rows, w[...]).astype(out.dtype)
    for xb in range(NX):
        k = lax.rem(xb - s[0] + NX, NX)
        for j in range(n + 1):
            at = j * HALF + xb * SUB
            out[k, j * SUB:(j + 1) * SUB, :] = acc[at:at + SUB, :]


def first(place, dy, low, high, w, flip):
    ff, width = w.shape
    n = dy.shape[0]
    rows = NZ * SUB
    far = pl.BlockSpec((HALF, width), lambda i, s: (0, 0))
    return pl.pallas_call(
        functools.partial(first_kernel, flip),
        grid_spec=pltpu.PrefetchScalarGridSpec(
            num_scalar_prefetch=1,
            grid=(1,),
            in_specs=[
                pl.BlockSpec((n, HALF, width), lambda i, s: (0, lax.rem(s[1] + flip, NC), 0)),
                far,
                far,
                pl.BlockSpec((ff, width), lambda i, s: (0, 0)),
            ],
            out_specs=pl.BlockSpec((NX, rows, ff), lambda i, s: (0, 0, 0)),
        ),
        out_shape=jax.ShapeDtypeStruct((NX, rows, ff), BF if flip else F32),
        compiler_params=params(16),
        cost_estimate=cost(2 * NX * rows * ff * width, 2 * ff * width + 4 * NX * rows * (ff + width)),
        name="first",
    )(place, dy, low, high, w)


def total_kernel(own, r1, r2, r3, *refs):
    refs[-1][...] = (own[...] + r1[...].astype(F32) + r2[...].astype(F32) + r3[...].astype(F32)).astype(BF)


def total_of(own, parts, *after):
    return pl.pallas_call(
        total_kernel,
        in_specs=[VMEM] * 4 + [HBM] * len(after),
        out_specs=VMEM,
        out_shape=jax.ShapeDtypeStruct(own.shape, BF),
        compiler_params=params(4),
        cost_estimate=cost(3 * own.size, 12 * own.size),
        name="total",
    )(own, *parts, *after)


def add_kernel(own, theirs, mine, s1, s2, s3):
    mine[...] = own[0] + theirs[0].astype(F32)
    for k, out in enumerate((s1, s2, s3), 1):
        out[...] = (own[k] + theirs[k].astype(F32)).astype(BF)


def pair_sums(own, theirs):
    shape = own.shape[1:]
    return pl.pallas_call(
        add_kernel,
        in_specs=[VMEM, VMEM],
        out_specs=[VMEM] * 4,
        out_shape=[jax.ShapeDtypeStruct(shape, F32)] + [jax.ShapeDtypeStruct(shape, BF)] * 3,
        compiler_params=params(6),
        cost_estimate=cost(own.size, 9 * own.size),
        name="pair",
    )(own, theirs)


def prep_kernel(s, mine, other, after, hidden_t, a_out, b_out, mark):
    y = s[3]
    same = lax.rem(lax.rem(s[2] + s[4 + pl.program_id(0)], NZ), NC) == s[1]

    def turned(i):
        rows = [pl.ds(pl.multiple_of(lax.rem(y + j, NY) * TOK, TOK), TOK) for j in range(NY)]
        got = [jnp.where(same, mine[0, i, r, :], other[0, i, r, :]) for r in rows]
        return jnp.concatenate(got, axis=0).astype(F32)

    g, u = turned(0), turned(1)
    sig = 1.0 / (1.0 + jnp.exp(-g))
    gs = g * sig
    a_out[...] = gs
    b_out[...] = u * sig * (1.0 + g * (1.0 - sig))
    hidden_t[...] = (gs * u).astype(BF).T
    mark[...] = jnp.zeros(mark.shape, F32)


def prep(place, mine, other, after):
    ff = mine.shape[-1]
    tokens = NZ * BLK
    rows = pl.BlockSpec((BLK, ff), lambda t, s: (t, 0))

    def piece(t, s):
        block = lax.rem(s[2] + s[4 + t], NZ)
        return (lax.rem(lax.div(block, NC) - s[0] + NX, NX), 0, 0, 0)

    spec = pl.BlockSpec((1, 2, BLK, ff), piece)
    return pl.pallas_call(
        prep_kernel,
        grid_spec=pltpu.PrefetchScalarGridSpec(
            num_scalar_prefetch=1,
            grid=(NZ,),
            in_specs=[spec, spec, HBM],
            out_specs=[
                pl.BlockSpec((ff, BLK), lambda t, s: (0, t)),
                rows,
                rows,
                pl.BlockSpec((8, 128), lambda t, s: (0, 0)),
            ],
        ),
        out_shape=[
            jax.ShapeDtypeStruct((ff, tokens), BF),
            jax.ShapeDtypeStruct((tokens, ff), F32),
            jax.ShapeDtypeStruct((tokens, ff), F32),
            jax.ShapeDtypeStruct((8, 128), F32),
        ],
        compiler_params=params(8),
        cost_estimate=cost(30 * tokens * ff, 14 * tokens * ff),
        name="prep",
    )(place, mine, other, after)


def turn_kernel(s, x_in, after, x_out, mark):
    rows = [pl.ds(pl.multiple_of(lax.rem(s[3] + j, NY) * TOK, TOK), TOK) for j in range(NY)]
    x_out[...] = jnp.concatenate([x_in[r, :] for r in rows], axis=0).T
    mark[...] = jnp.zeros(mark.shape, F32)


def turn(place, x_all, after):
    tokens, width = x_all.shape
    return pl.pallas_call(
        turn_kernel,
        grid_spec=pltpu.PrefetchScalarGridSpec(
            num_scalar_prefetch=1,
            grid=(NZ,),
            in_specs=[pl.BlockSpec((BLK, width), lambda t, s: (lax.rem(s[2] + s[4 + t], NZ), 0)), HBM],
            out_specs=[
                pl.BlockSpec((width, BLK), lambda t, s: (0, t)),
                pl.BlockSpec((8, 128), lambda t, s: (0, 0)),
            ],
        ),
        out_shape=[jax.ShapeDtypeStruct((width, tokens), BF), jax.ShapeDtypeStruct((8, 128), F32)],
        compiler_params=params(8),
        cost_estimate=cost(0, 4 * tokens * width),
        name="turn",
    )(place, x_all, after)


def second_kernel(s, mine, other, a, b, gw, uw, dg, du, p):
    for j in range(dg.shape[0] // BLK):
        here = slice(j * SUB, (j + 1) * SUB)
        for half in range(NC):
            for xb in range(NX):
                k = lax.rem(xb - s[0] + NX, NX)
                d = jnp.where(s[1] == half, mine[k, here, :], other[k, here, :]).astype(F32)
                at = j * BLK + half * HALF + xb * SUB
                rows = slice(at, at + SUB)
                du[rows, :] = (d * a[rows, :]).astype(BF)
                dg[rows, :] = (d * b[rows, :]).astype(BF)
    p[...] = (nt(dg[...], gw[...]) + nt(du[...], uw[...])).astype(BF)


def second(place, mine, other, a, b, gate_weight, up_weight):
    tokens, ff = a.shape
    width = gate_weight.shape[0]
    tile = 4 * BLK
    got = pl.BlockSpec((NX, 4 * SUB, ff), lambda t, s: (0, t, 0))
    row = pl.BlockSpec((tile, ff), lambda t, s: (t, 0))
    whole = pl.BlockSpec((width, ff), lambda t, s: (0, 0))
    return pl.pallas_call(
        second_kernel,
        grid_spec=pltpu.PrefetchScalarGridSpec(
            num_scalar_prefetch=1,
            grid=(tokens // tile,),
            in_specs=[got, got, row, row, whole, whole],
            out_specs=[row, row, pl.BlockSpec((tile, width), lambda t, s: (t, 0))],
        ),
        out_shape=[
            pltpu.HBM((tokens, ff), BF),
            pltpu.HBM((tokens, ff), BF),
            jax.ShapeDtypeStruct((tokens, width), BF),
        ],
        compiler_params=params(30),
        cost_estimate=cost(4 * tokens * ff * width, 16 * tokens * ff + 4 * ff * width),
        name="second",
    )(place, mine, other, a, b, gate_weight, up_weight)


def product_kernel(n, a, *refs):
    parts, (after, out, mark) = refs[:n], refs[n:]
    b = jnp.concatenate([v[...] for v in parts], axis=0)
    out[...] = jnp.dot(a[...], b, preferred_element_type=F32).astype(BF)
    mark[...] = jnp.zeros(mark.shape, F32)


def product(a, parts, tile, after):
    m, k = a.shape
    n = parts[0].shape[1]
    return pl.pallas_call(
        functools.partial(product_kernel, len(parts)),
        grid=(m // tile,),
        in_specs=[pl.BlockSpec((tile, k), lambda i: (i, 0))]
        + [pl.BlockSpec(v.shape, lambda i: (0, 0)) for v in parts]
        + [HBM],
        out_specs=[pl.BlockSpec((tile, n), lambda i: (i, 0)), pl.BlockSpec((8, 128), lambda i: (0, 0))],
        out_shape=[jax.ShapeDtypeStruct((m, n), BF), jax.ShapeDtypeStruct((8, 128), F32)],
        compiler_params=params(16),
        cost_estimate=cost(2 * m * k * n, 2 * (m * k + k * n + m * n)),
        name="product",
    )(a, *parts, after)


def near_kernel(bu, bd, up, down, *refs):
    up_out, down_out = refs[-2:]
    up_out[:HALF, :] = (bu[:HALF, :].astype(F32) + up[...].astype(F32)).astype(BF)
    up_out[HALF:, :] = bu[HALF:, :]
    down_out[:HALF, :] = bd[:HALF, :]
    down_out[HALF:, :] = (bd[HALF:, :].astype(F32) + down[...].astype(F32)).astype(BF)


def step_kernel(bu, bd, up, down, *refs):
    up_out, down_out = refs[-2:]
    up_out[...] = (bu[...].astype(F32) + up[...].astype(F32)).astype(BF)
    down_out[...] = (bd[...].astype(F32) + down[...].astype(F32)).astype(BF)


def step(kernel, p, i, j, up, down, *after):
    width = p.shape[1]
    sds = jax.ShapeDtypeStruct((BLK, width), BF)
    whole = pl.BlockSpec(up.shape, lambda t: (0, 0))
    block = pl.BlockSpec((BLK, width), lambda t: (0, 0))
    return pl.pallas_call(
        kernel,
        grid=(1,),
        in_specs=[
            pl.BlockSpec((BLK, width), lambda t: (i, 0)),
            pl.BlockSpec((BLK, width), lambda t: (j, 0)),
            whole,
            whole,
        ]
        + [HBM] * len(after),
        out_specs=[block, block],
        out_shape=[sds, sds],
        compiler_params=params(6),
        cost_estimate=cost(2 * BLK * width, 12 * BLK * width),
        name="step",
    )(p, p, up, down, *after)


def own_kernel(b0, up, down, after, own, s1, s2, s3):
    total = b0[...].astype(F32) + up[...].astype(F32) + down[...].astype(F32)
    own[...] = total[:TOK, :]
    for k, out in enumerate((s1, s2, s3), 1):
        out[...] = total[k * TOK:(k + 1) * TOK, :].astype(BF)


def own_of(p, up, down, after):
    width = p.shape[1]
    block = pl.BlockSpec((BLK, width), lambda t: (0, 0))
    out = pl.BlockSpec((TOK, width), lambda t: (0, 0))
    return pl.pallas_call(
        own_kernel,
        grid=(1,),
        in_specs=[block] * 3 + [HBM],
        out_specs=[out] * 4,
        out_shape=[jax.ShapeDtypeStruct((TOK, width), F32)] + [jax.ShapeDtypeStruct((TOK, width), BF)] * 3,
        compiler_params=params(6),
        cost_estimate=cost(2 * BLK * width, 8 * BLK * width),
        name="own",
    )(p, up, down, after)


def scatter_z_y(p, marks):
    last = p[7 * BLK:]
    up, down = from_z(last[:HALF], -1), from_z(last[HALF:], 1)
    up, down = step(near_kernel, p, 3, 4, up, down, *marks[0])
    for n, i, j in ((1, 2, 5), (2, 1, 6)):
        up, down = step(step_kernel, p, i, j, from_z(up, -1), from_z(down, 1), marks[n])
    own, *sent = own_of(p, from_z(up, -1), from_z(down, 1), marks[3])
    return total_of(own, [from_y(v, -k) for k, v in enumerate(sent, 1)])


def on_device(
    inputs,
    cotangent,
    gate_pre,
    up_pre,
    gate_weight,
    up_weight,
    down_weight,
    pair_ids,
    flags,
    pair_scale,
):
    row, col = lax.axis_index("row"), lax.axis_index("col")
    place = jnp.stack([row // NC, row % NC, col // NY, col % NY] + [jnp.int32(t) for t in ORDER])
    place = place.astype(jnp.int32)
    scaled = weigh(cotangent, pair_ids, flags, pair_scale)
    x_all = lax.all_gather(inputs, "col", axis=0, tiled=True)

    dy0, pre = lead([scaled] + [from_y(scaled, k) for k in range(1, NY)], gate_pre, up_pre)
    up, down = [dy0], [dy0]
    for _ in range(3):
        up.append(from_z(up[-1], 1))
        down.append(from_z(down[-1], -1))
    pre_parts = [from_x(pre, k) for k in range(1, NX)]
    low, high = halves(up[3], down[3], pre_parts)
    low, high = from_z(low, 1), from_z(high, -1)
    dy = jnp.stack(up + [down[3], down[2], down[1]], axis=0)
    pre_mine = jnp.stack([pre] + pre_parts, axis=0)
    pre_other = from_core(pre_mine)

    sent = first(place, dy, low, high, down_weight, 1)
    hidden_t, a, b, ready = prep(place, pre_mine, pre_other, sent)
    own, *parts = pair_sums(first(place, dy, low, high, down_weight, 0), from_core(sent))
    total = total_of(own, [from_x(v, -k) for k, v in enumerate(parts, 1)], ready)
    mine = jnp.stack([total] + [from_x(total, k) for k in range(1, NX)], axis=0)
    d_gate, d_up, part = second(place, mine, from_core(mine), a, b, gate_weight, up_weight)

    flat = dy.reshape(-1, dy.shape[2])
    grad_down, mark_0 = product(hidden_t, [flat, low, high], 448, part[:8, :128])
    x_t, mark_1 = turn(place, x_all, mark_0)
    grad_gate, mark_2 = product(x_t, [d_gate], 512, mark_1)
    grad_up, mark_3 = product(x_t, [d_up], 512, mark_2)
    grad_input = scatter_z_y(part, ((mark_0, x_all[:16, :128]), mark_1, mark_2, mark_3))
    return (grad_input, grad_gate, grad_up, grad_down)


def solution(mesh):
    return jax.shard_map(
        on_device,
        mesh=mesh,
        in_specs=(
            P("col", "row"),
            P("col", "row"),
            P("row", "col"),
            P("row", "col"),
            P("row", "col"),
            P("row", "col"),
            P("col", "row"),
            P("col"),
            P("col"),
            P(),
        ),
        out_specs=(P("col", "row"), P("row", "col"), P("row", "col"), P("col", "row")),
        check_vma=False,
    )
```

```python
import functools

import jax
import jax.numpy as jnp
from jax import lax
from jax.experimental import pallas as pl
from jax.experimental.pallas import tpu as pltpu
from jax.sharding import PartitionSpec as P

NX, NC, NZ, NY = 4, 2, 8, 4
TOK = 32
BLK = NY * TOK
HALF = BLK // NC
SUB = HALF // NX
ORDER = (0, 1, 2, 3, 5, 6, 7, 4)
BF, F32 = jnp.bfloat16, jnp.float32
HBM = pl.BlockSpec(memory_space=pltpu.HBM)
VMEM = pl.BlockSpec(memory_space=pltpu.VMEM)
SMEM = pl.BlockSpec(memory_space=pltpu.SMEM)


def stay(v):
    return pltpu.with_memory_space_constraint(v, pltpu.HBM)


def params(mib):
    return pltpu.CompilerParams(vmem_limit_bytes=mib << 20)


def cost(flops, size):
    return pl.CostEstimate(flops=flops, bytes_accessed=size, transcendentals=0)


def from_z(v, k):
    perm = [(z * NY + y, (z - k) % NZ * NY + y) for z in range(NZ) for y in range(NY)]
    return lax.ppermute(v, "col", perm)


def from_y(v, k):
    perm = [(z * NY + y, z * NY + (y - k) % NY) for z in range(NZ) for y in range(NY)]
    return lax.ppermute(v, "col", perm)


def from_x(v, k):
    perm = [(x * NC + c, (x - k) % NX * NC + c) for x in range(NX) for c in range(NC)]
    return lax.ppermute(v, "row", perm)


def from_core(v):
    return lax.ppermute(v, "row", [(r, r ^ 1) for r in range(NX * NC)])


def weigh_kernel(ids_in, flags_in, scale_in, cot_in, out, ids, flags, scale, cot, sems):
    copies = [
        pltpu.make_async_copy(src, dst, sems.at[i])
        for i, (src, dst) in enumerate(
            ((ids_in, ids), (flags_in, flags), (scale_in, scale), (cot_in, cot))
        )
    ]
    for copy in copies:
        copy.start()
    for copy in copies:
        copy.wait()
    row = lax.broadcasted_iota(jnp.int32, cot.shape, 0)
    weight = jnp.zeros(cot.shape, F32)
    for r in range(TOK):
        w = (2 * flags[r] - 1).astype(F32) * scale[ids[r]]
        weight = jnp.where(row == r, w, weight)
    out[...] = (cot[...].astype(F32) * weight).astype(BF)


def weigh(cotangent, pair_ids, flags, pair_scale):
    return pl.pallas_call(
        weigh_kernel,
        in_specs=[HBM] * 4,
        out_specs=VMEM,
        out_shape=jax.ShapeDtypeStruct(cotangent.shape, BF),
        scratch_shapes=[
            pltpu.SMEM(pair_ids.shape, jnp.int32),
            pltpu.SMEM(flags.shape, jnp.int32),
            pltpu.SMEM(pair_scale.shape, F32),
            pltpu.VMEM(cotangent.shape, BF),
            pltpu.SemaphoreType.DMA((4,)),
        ],
        compiler_params=params(4),
        cost_estimate=cost(cotangent.size, 8 * cotangent.size),
        name="weigh",
    )(*map(stay, (pair_ids, flags, pair_scale, cotangent)))


def pack_kernel(g, u, after, pre, sems):
    copies = [pltpu.make_async_copy(v, pre.at[i], sems.at[i]) for i, v in enumerate((g, u))]
    for copy in copies:
        copy.start()
    for copy in copies:
        copy.wait()


def pack(gate_pre, up_pre, after):
    return pl.pallas_call(
        pack_kernel,
        in_specs=[HBM] * 3,
        out_specs=VMEM,
        out_shape=jax.ShapeDtypeStruct((2,) + gate_pre.shape, BF),
        scratch_shapes=[pltpu.SemaphoreType.DMA((2,))],
        compiler_params=params(4),
        cost_estimate=cost(0, 8 * gate_pre.size),
        name="pack",
    )(stay(gate_pre), stay(up_pre), after)


def halves_kernel(u, d, r1, r2, low, high):
    low[...] = u[:HALF, :]
    high[...] = d[HALF:, :]


def halves(u, d, after):
    half = jax.ShapeDtypeStruct((HALF, u.shape[1]), BF)
    return pl.pallas_call(
        halves_kernel,
        in_specs=[VMEM] * 2 + [HBM] * 2,
        out_specs=[VMEM] * 2,
        out_shape=[half, half],
        compiler_params=params(4),
        cost_estimate=cost(0, 4 * u.size),
        name="halves",
    )(u, d, *after)


def nt(a, b):
    return lax.dot_general(a, b, (((1,), (1,)), ((), ())), preferred_element_type=F32)


def first_kernel(flip, s, dy, low, high, w, out):
    n = dy.shape[0]
    far = jnp.where(lax.rem(s[1] + flip, NC) == 0, low[...], high[...])
    rows = jnp.concatenate([dy[j] for j in range(n)] + [far], axis=0)
    acc = nt(rows, w[...]).astype(out.dtype)
    for xb in range(NX):
        k = lax.rem(xb - s[0] + NX, NX)
        for j in range(n + 1):
            at = j * HALF + xb * SUB
            out[k, j * SUB:(j + 1) * SUB, :] = acc[at:at + SUB, :]


def first(place, dy, low, high, w, flip):
    ff, width = w.shape
    n = dy.shape[0]
    rows = NZ * SUB
    far = pl.BlockSpec((HALF, width), lambda i, s: (0, 0))
    return pl.pallas_call(
        functools.partial(first_kernel, flip),
        grid_spec=pltpu.PrefetchScalarGridSpec(
            num_scalar_prefetch=1,
            grid=(1,),
            in_specs=[
                pl.BlockSpec((n, HALF, width), lambda i, s: (0, lax.rem(s[1] + flip, NC), 0)),
                far,
                far,
                pl.BlockSpec((ff, width), lambda i, s: (0, 0)),
            ],
            out_specs=pl.BlockSpec((NX, rows, ff), lambda i, s: (0, 0, 0)),
        ),
        out_shape=jax.ShapeDtypeStruct((NX, rows, ff), BF if flip else F32),
        compiler_params=params(16),
        cost_estimate=cost(2 * NX * rows * ff * width, 2 * ff * width + 4 * NX * rows * (ff + width)),
        name="first",
    )(place, dy, low, high, w)


def total_kernel(own, r1, r2, r3, *refs):
    refs[-1][...] = (own[...] + r1[...].astype(F32) + r2[...].astype(F32) + r3[...].astype(F32)).astype(BF)


def total_of(own, parts, *after):
    return pl.pallas_call(
        total_kernel,
        in_specs=[VMEM] * 4 + [HBM] * len(after),
        out_specs=VMEM,
        out_shape=jax.ShapeDtypeStruct(own.shape, BF),
        compiler_params=params(4),
        cost_estimate=cost(3 * own.size, 12 * own.size),
        name="total",
    )(own, *parts, *after)


def join_kernel(a, b, c, d, after, out):
    for k, v in enumerate((a, b, c, d)):
        out[k] = v[...]


def join(parts, after):
    shape = parts[0].shape
    return pl.pallas_call(
        join_kernel,
        in_specs=[VMEM] * 4 + [HBM],
        out_specs=VMEM,
        out_shape=jax.ShapeDtypeStruct((NX,) + shape, BF),
        compiler_params=params(4),
        cost_estimate=cost(0, 16 * parts[0].size),
        name="join",
    )(*parts, after)


def add_kernel(own, theirs, mine, s1, s2, s3):
    mine[...] = own[0] + theirs[0].astype(F32)
    for k, out in enumerate((s1, s2, s3), 1):
        out[...] = (own[k] + theirs[k].astype(F32)).astype(BF)


def pair_sums(own, theirs):
    shape = own.shape[1:]
    return pl.pallas_call(
        add_kernel,
        in_specs=[VMEM, VMEM],
        out_specs=[VMEM] * 4,
        out_shape=[jax.ShapeDtypeStruct(shape, F32)] + [jax.ShapeDtypeStruct(shape, BF)] * 3,
        compiler_params=params(6),
        cost_estimate=cost(own.size, 9 * own.size),
        name="pair",
    )(own, theirs)


def prep_kernel(s, mine, other, after, hidden_t, a_out, b_out, mark):
    y = s[3]
    same = lax.rem(lax.rem(s[2] + s[4 + pl.program_id(0)], NZ), NC) == s[1]

    def turned(i):
        rows = [pl.ds(pl.multiple_of(lax.rem(y + j, NY) * TOK, TOK), TOK) for j in range(NY)]
        got = [jnp.where(same, mine[0, i, r, :], other[0, i, r, :]) for r in rows]
        return jnp.concatenate(got, axis=0).astype(F32)

    g, u = turned(0), turned(1)
    sig = 1.0 / (1.0 + jnp.exp(-g))
    gs = g * sig
    a_out[...] = gs
    b_out[...] = u * sig * (1.0 + g * (1.0 - sig))
    hidden_t[...] = (gs * u).astype(BF).T
    mark[...] = jnp.zeros(mark.shape, F32)


def prep(place, mine, other, after):
    ff = mine.shape[-1]
    tokens = NZ * BLK
    rows = pl.BlockSpec((BLK, ff), lambda t, s: (t, 0))

    def piece(t, s):
        block = lax.rem(s[2] + s[4 + t], NZ)
        return (lax.rem(lax.div(block, NC) - s[0] + NX, NX), 0, 0, 0)

    spec = pl.BlockSpec((1, 2, BLK, ff), piece)
    return pl.pallas_call(
        prep_kernel,
        grid_spec=pltpu.PrefetchScalarGridSpec(
            num_scalar_prefetch=1,
            grid=(NZ,),
            in_specs=[spec, spec, HBM],
            out_specs=[
                pl.BlockSpec((ff, BLK), lambda t, s: (0, t)),
                rows,
                rows,
                pl.BlockSpec((8, 128), lambda t, s: (0, 0)),
            ],
        ),
        out_shape=[
            jax.ShapeDtypeStruct((ff, tokens), BF),
            jax.ShapeDtypeStruct((tokens, ff), F32),
            jax.ShapeDtypeStruct((tokens, ff), F32),
            jax.ShapeDtypeStruct((8, 128), F32),
        ],
        compiler_params=params(8),
        cost_estimate=cost(30 * tokens * ff, 14 * tokens * ff),
        name="prep",
    )(place, mine, other, after)


def turn_kernel(s, x_in, after, x_out, mark):
    rows = [pl.ds(pl.multiple_of(lax.rem(s[3] + j, NY) * TOK, TOK), TOK) for j in range(NY)]
    x_out[...] = jnp.concatenate([x_in[r, :] for r in rows], axis=0).T
    mark[...] = jnp.zeros(mark.shape, F32)


def turn(place, x_all, after):
    tokens, width = x_all.shape
    return pl.pallas_call(
        turn_kernel,
        grid_spec=pltpu.PrefetchScalarGridSpec(
            num_scalar_prefetch=1,
            grid=(NZ,),
            in_specs=[pl.BlockSpec((BLK, width), lambda t, s: (lax.rem(s[2] + s[4 + t], NZ), 0)), HBM],
            out_specs=[
                pl.BlockSpec((width, BLK), lambda t, s: (0, t)),
                pl.BlockSpec((8, 128), lambda t, s: (0, 0)),
            ],
        ),
        out_shape=[jax.ShapeDtypeStruct((width, tokens), BF), jax.ShapeDtypeStruct((8, 128), F32)],
        compiler_params=params(8),
        cost_estimate=cost(0, 4 * tokens * width),
        name="turn",
    )(place, x_all, after)


def second_kernel(s, mine, other, a, b, gw, uw, dg, du, p):
    for j in range(dg.shape[0] // BLK):
        here = slice(j * SUB, (j + 1) * SUB)
        for half in range(NC):
            for xb in range(NX):
                k = lax.rem(xb - s[0] + NX, NX)
                d = jnp.where(s[1] == half, mine[k, here, :], other[k, here, :]).astype(F32)
                at = j * BLK + half * HALF + xb * SUB
                rows = slice(at, at + SUB)
                du[rows, :] = (d * a[rows, :]).astype(BF)
                dg[rows, :] = (d * b[rows, :]).astype(BF)
    p[...] = (nt(dg[...], gw[...]) + nt(du[...], uw[...])).astype(BF)


def second(place, mine, other, a, b, gate_weight, up_weight, at, n):
    ff = a.shape[1]
    width = gate_weight.shape[0]
    rows = n * BLK

    def whole(*shape):
        return pl.BlockSpec(shape, lambda t, s: (0,) * len(shape))

    got = pl.BlockSpec((NX, n * SUB, ff), lambda t, s: (0, at // n, 0))
    row = pl.BlockSpec((rows, ff), lambda t, s: (at // n, 0))
    return pl.pallas_call(
        second_kernel,
        grid_spec=pltpu.PrefetchScalarGridSpec(
            num_scalar_prefetch=1,
            grid=(1,),
            in_specs=[got, got, row, row, whole(width, ff), whole(width, ff)],
            out_specs=[whole(rows, ff), whole(rows, ff), whole(rows, width)],
        ),
        out_shape=[
            pltpu.HBM((rows, ff), BF),
            pltpu.HBM((rows, ff), BF),
            jax.ShapeDtypeStruct((rows, width), BF),
        ],
        compiler_params=params(32),
        cost_estimate=cost(4 * rows * ff * width, 16 * rows * ff + 4 * ff * width),
        name="second",
    )(place, mine, other, a, b, gate_weight, up_weight)


def product_kernel(n, a, *refs):
    parts, (after, out, mark) = refs[:n], refs[n:]
    b = jnp.concatenate([v[...] for v in parts], axis=0)
    out[...] = jnp.dot(a[...], b, preferred_element_type=F32).astype(BF)
    mark[...] = jnp.zeros(mark.shape, F32)


def product(a, parts, tile, after):
    m, k = a.shape
    n = parts[0].shape[1]
    return pl.pallas_call(
        functools.partial(product_kernel, len(parts)),
        grid=(m // tile,),
        in_specs=[pl.BlockSpec((tile, k), lambda i: (i, 0))]
        + [pl.BlockSpec(v.shape, lambda i: (0, 0)) for v in parts]
        + [HBM],
        out_specs=[pl.BlockSpec((tile, n), lambda i: (i, 0)), pl.BlockSpec((8, 128), lambda i: (0, 0))],
        out_shape=[jax.ShapeDtypeStruct((m, n), BF), jax.ShapeDtypeStruct((8, 128), F32)],
        compiler_params=params(16),
        cost_estimate=cost(2 * m * k * n, 2 * (m * k + k * n + m * n)),
        name="product",
    )(a, *parts, after)


def near_kernel(bu, bd, up, down, *refs):
    up_out, down_out = refs[-2:]
    up_out[:HALF, :] = (bu[:HALF, :].astype(F32) + up[...].astype(F32)).astype(BF)
    up_out[HALF:, :] = bu[HALF:, :]
    down_out[:HALF, :] = bd[:HALF, :]
    down_out[HALF:, :] = (bd[HALF:, :].astype(F32) + down[...].astype(F32)).astype(BF)


def step_kernel(bu, bd, up, down, *refs):
    up_out, down_out = refs[-2:]
    up_out[...] = (bu[...].astype(F32) + up[...].astype(F32)).astype(BF)
    down_out[...] = (bd[...].astype(F32) + down[...].astype(F32)).astype(BF)


def step(kernel, p, i, j, up, down, *after):
    width = p.shape[1]
    sds = jax.ShapeDtypeStruct((BLK, width), BF)
    whole = pl.BlockSpec(up.shape, lambda t: (0, 0))
    block = pl.BlockSpec((BLK, width), lambda t: (0, 0))
    return pl.pallas_call(
        kernel,
        grid=(1,),
        in_specs=[
            pl.BlockSpec((BLK, width), lambda t: (i, 0)),
            pl.BlockSpec((BLK, width), lambda t: (j, 0)),
            whole,
            whole,
        ]
        + [HBM] * len(after),
        out_specs=[block, block],
        out_shape=[sds, sds],
        compiler_params=params(6),
        cost_estimate=cost(2 * BLK * width, 12 * BLK * width),
        name="step",
    )(p, p, up, down, *after)


def own_kernel(b0, up, down, after, own, s1, s2, s3):
    total = b0[...].astype(F32) + up[...].astype(F32) + down[...].astype(F32)
    own[...] = total[:TOK, :]
    for k, out in enumerate((s1, s2, s3), 1):
        out[...] = total[k * TOK:(k + 1) * TOK, :].astype(BF)


def own_of(p, up, down, after):
    width = p.shape[1]
    block = pl.BlockSpec((BLK, width), lambda t: (0, 0))
    out = pl.BlockSpec((TOK, width), lambda t: (0, 0))
    return pl.pallas_call(
        own_kernel,
        grid=(1,),
        in_specs=[block] * 3 + [HBM],
        out_specs=[out] * 4,
        out_shape=[jax.ShapeDtypeStruct((TOK, width), F32)] + [jax.ShapeDtypeStruct((TOK, width), BF)] * 3,
        compiler_params=params(6),
        cost_estimate=cost(2 * BLK * width, 8 * BLK * width),
        name="own",
    )(p, up, down, after)


def scatter_z_y(p, ends, marks):
    up, down = step(near_kernel, p, 3, 4, *ends, *marks[0])
    for n, i, j in ((1, 2, 5), (2, 1, 6)):
        up, down = step(step_kernel, p, i, j, from_z(up, -1), from_z(down, 1), marks[n])
    own, *sent = own_of(p, from_z(up, -1), from_z(down, 1), marks[3])
    return total_of(own, [from_y(v, -k) for k, v in enumerate(sent, 1)])


def on_device(
    inputs,
    cotangent,
    gate_pre,
    up_pre,
    gate_weight,
    up_weight,
    down_weight,
    pair_ids,
    flags,
    pair_scale,
):
    row, col = lax.axis_index("row"), lax.axis_index("col")
    place = jnp.stack([row // NC, row % NC, col // NY, col % NY] + [jnp.int32(t) for t in ORDER])
    place = place.astype(jnp.int32)
    scaled = weigh(cotangent, pair_ids, flags, pair_scale)
    x_all = lax.all_gather(inputs, "col", axis=0, tiled=True)

    dy0 = jnp.concatenate([scaled] + [from_y(scaled, k) for k in range(1, NY)], axis=0)
    pre = pack(gate_pre, up_pre, scaled)
    up, down = [dy0], [dy0]
    for _ in range(3):
        up.append(from_z(up[-1], 1))
        down.append(from_z(down[-1], -1))
    next_pre, last_pre = from_x(pre, 1), from_x(pre, -1)
    far_pre = from_x(next_pre[0], 1), from_x(last_pre[1], -1)
    low, high = halves(up[3], down[3], far_pre)
    low, high = from_z(low, 1), from_z(high, -1)
    dy = jnp.stack(up + [down[3], down[2], down[1]], axis=0)
    pre_mine = jnp.stack([pre, next_pre, jnp.stack(far_pre, axis=0), last_pre], axis=0)
    pre_other = from_core(pre_mine)

    sent = first(place, dy, low, high, down_weight, 1)
    hidden_t, a, b, ready = prep(place, pre_mine, pre_other, sent)
    own, *parts = pair_sums(first(place, dy, low, high, down_weight, 0), from_core(sent))
    total = total_of(own, [from_x(v, -k) for k, v in enumerate(parts, 1)], ready)
    flat = dy.reshape(-1, dy.shape[2])
    grad_down, mark_0 = product(hidden_t, [flat, low, high], 448, total)
    mine = join([total] + [from_x(total, k) for k in range(1, NX)], mark_0)
    args = place, mine, from_core(mine), a, b, gate_weight, up_weight
    far = second(*args, NZ - 1, 1)
    last = far[2]
    ends = from_z(last[:HALF], -1), from_z(last[HALF:], 1)
    near = second(*args, 0, NZ - 1)
    d_gate, d_up, part = zip(near, far)

    x_t, mark_1 = turn(place, x_all, near[2])
    grad_gate, mark_2 = product(x_t, d_gate, 512, mark_1)
    grad_up, mark_3 = product(x_t, d_up, 512, mark_2)
    grad_input = scatter_z_y(near[2], ends, ((x_all[:16, :128],), mark_1, mark_2, mark_3))
    return (grad_input, grad_gate, grad_up, grad_down)


def solution(mesh):
    return jax.shard_map(
        on_device,
        mesh=mesh,
        in_specs=(
            P("col", "row"),
            P("col", "row"),
            P("row", "col"),
            P("row", "col"),
            P("row", "col"),
            P("row", "col"),
            P("col", "row"),
            P("col"),
            P("col"),
            P(),
        ),
        out_specs=(P("col", "row"), P("row", "col"), P("row", "col"), P("col", "row")),
        check_vma=False,
    )
```

```python
import functools

import jax
import jax.numpy as jnp
from jax import lax
from jax.experimental import pallas as pl
from jax.experimental.pallas import tpu as pltpu
from jax.sharding import PartitionSpec as P

NX, NC, NZ, NY = 4, 2, 8, 4
TOK = 32
BLK = NY * TOK
HALF = BLK // NC
SUB = HALF // NX
ORDER = (0, 1, 2, 6, 7, 3, 5, 4)
BF, F32 = jnp.bfloat16, jnp.float32
HBM = pl.BlockSpec(memory_space=pltpu.HBM)
VMEM = pl.BlockSpec(memory_space=pltpu.VMEM)
SMEM = pl.BlockSpec(memory_space=pltpu.SMEM)


def stay(v):
    return pltpu.with_memory_space_constraint(v, pltpu.HBM)


def params(mib):
    return pltpu.CompilerParams(vmem_limit_bytes=mib << 20)


def cost(flops, size):
    return pl.CostEstimate(flops=flops, bytes_accessed=size, transcendentals=0)


def from_z(v, k):
    perm = [(z * NY + y, (z - k) % NZ * NY + y) for z in range(NZ) for y in range(NY)]
    return lax.ppermute(v, "col", perm)


def from_y(v, k):
    perm = [(z * NY + y, z * NY + (y - k) % NY) for z in range(NZ) for y in range(NY)]
    return lax.ppermute(v, "col", perm)


def from_x(v, k):
    perm = [(x * NC + c, (x - k) % NX * NC + c) for x in range(NX) for c in range(NC)]
    return lax.ppermute(v, "row", perm)


def from_core(v):
    return lax.ppermute(v, "row", [(r, r ^ 1) for r in range(NX * NC)])


def weigh_kernel(ids_in, flags_in, scale_in, cot_in, out, ids, flags, scale, cot, sems):
    copies = [
        pltpu.make_async_copy(src, dst, sems.at[i])
        for i, (src, dst) in enumerate(
            ((ids_in, ids), (flags_in, flags), (scale_in, scale), (cot_in, cot))
        )
    ]
    for copy in copies:
        copy.start()
    for copy in copies:
        copy.wait()
    row = lax.broadcasted_iota(jnp.int32, cot.shape, 0)
    weight = jnp.zeros(cot.shape, F32)
    for r in range(TOK):
        w = (2 * flags[r] - 1).astype(F32) * scale[ids[r]]
        weight = jnp.where(row == r, w, weight)
    out[...] = (cot[...].astype(F32) * weight).astype(BF)


def weigh(cotangent, pair_ids, flags, pair_scale):
    return pl.pallas_call(
        weigh_kernel,
        in_specs=[HBM] * 4,
        out_specs=VMEM,
        out_shape=jax.ShapeDtypeStruct(cotangent.shape, BF),
        scratch_shapes=[
            pltpu.SMEM(pair_ids.shape, jnp.int32),
            pltpu.SMEM(flags.shape, jnp.int32),
            pltpu.SMEM(pair_scale.shape, F32),
            pltpu.VMEM(cotangent.shape, BF),
            pltpu.SemaphoreType.DMA((4,)),
        ],
        compiler_params=params(4),
        cost_estimate=cost(cotangent.size, 8 * cotangent.size),
        name="weigh",
    )(*map(stay, (pair_ids, flags, pair_scale, cotangent)))


def pack_kernel(g, u, after, pre, sems):
    copies = [pltpu.make_async_copy(v, pre.at[i], sems.at[i]) for i, v in enumerate((g, u))]
    for copy in copies:
        copy.start()
    for copy in copies:
        copy.wait()


def pack(gate_pre, up_pre, after):
    return pl.pallas_call(
        pack_kernel,
        in_specs=[HBM] * 3,
        out_specs=VMEM,
        out_shape=jax.ShapeDtypeStruct((2,) + gate_pre.shape, BF),
        scratch_shapes=[pltpu.SemaphoreType.DMA((2,))],
        compiler_params=params(4),
        cost_estimate=cost(0, 8 * gate_pre.size),
        name="pack",
    )(stay(gate_pre), stay(up_pre), after)


def halves_kernel(u, d, r1, r2, low, high):
    low[...] = u[:HALF, :]
    high[...] = d[HALF:, :]


def halves(u, d, after):
    half = jax.ShapeDtypeStruct((HALF, u.shape[1]), BF)
    return pl.pallas_call(
        halves_kernel,
        in_specs=[VMEM] * 2 + [HBM] * 2,
        out_specs=[VMEM] * 2,
        out_shape=[half, half],
        compiler_params=params(4),
        cost_estimate=cost(0, 4 * u.size),
        name="halves",
    )(u, d, *after)


def nt(a, b):
    return lax.dot_general(a, b, (((1,), (1,)), ((), ())), preferred_element_type=F32)


def first_kernel(flip, s, dy, low, high, w, out):
    n = dy.shape[0]
    far = jnp.where(lax.rem(s[1] + flip, NC) == 0, low[...], high[...])
    rows = jnp.concatenate([dy[j] for j in range(n)] + [far], axis=0)
    acc = nt(rows, w[...]).astype(out.dtype)
    for xb in range(NX):
        k = lax.rem(xb - s[0] + NX, NX)
        for j in range(n + 1):
            at = j * HALF + xb * SUB
            out[k, j * SUB:(j + 1) * SUB, :] = acc[at:at + SUB, :]


def first(place, dy, low, high, w, flip):
    ff, width = w.shape
    n = dy.shape[0]
    rows = NZ * SUB
    far = pl.BlockSpec((HALF, width), lambda i, s: (0, 0))
    return pl.pallas_call(
        functools.partial(first_kernel, flip),
        grid_spec=pltpu.PrefetchScalarGridSpec(
            num_scalar_prefetch=1,
            grid=(1,),
            in_specs=[
                pl.BlockSpec((n, HALF, width), lambda i, s: (0, lax.rem(s[1] + flip, NC), 0)),
                far,
                far,
                pl.BlockSpec((ff, width), lambda i, s: (0, 0)),
            ],
            out_specs=pl.BlockSpec((NX, rows, ff), lambda i, s: (0, 0, 0)),
        ),
        out_shape=jax.ShapeDtypeStruct((NX, rows, ff), BF if flip else F32),
        compiler_params=params(16),
        cost_estimate=cost(2 * NX * rows * ff * width, 2 * ff * width + 4 * NX * rows * (ff + width)),
        name="first",
    )(place, dy, low, high, w)


def total_kernel(own, r1, r2, r3, *refs):
    refs[-1][...] = (own[...] + r1[...].astype(F32) + r2[...].astype(F32) + r3[...].astype(F32)).astype(BF)


def total_of(own, parts, *after):
    return pl.pallas_call(
        total_kernel,
        in_specs=[VMEM] * 4 + [HBM] * len(after),
        out_specs=VMEM,
        out_shape=jax.ShapeDtypeStruct(own.shape, BF),
        compiler_params=params(4),
        cost_estimate=cost(3 * own.size, 12 * own.size),
        name="total",
    )(own, *parts, *after)


def join_kernel(a, b, c, d, after, out):
    for k, v in enumerate((a, b, c, d)):
        out[k] = v[...]


def join(parts, after):
    shape = parts[0].shape
    return pl.pallas_call(
        join_kernel,
        in_specs=[VMEM] * 4 + [HBM],
        out_specs=VMEM,
        out_shape=jax.ShapeDtypeStruct((NX,) + shape, BF),
        compiler_params=params(4),
        cost_estimate=cost(0, 16 * parts[0].size),
        name="join",
    )(*parts, after)


def add_kernel(own, theirs, mine, s1, s2, s3):
    mine[...] = own[0] + theirs[0].astype(F32)
    for k, out in enumerate((s1, s2, s3), 1):
        out[...] = (own[k] + theirs[k].astype(F32)).astype(BF)


def pair_sums(own, theirs):
    shape = own.shape[1:]
    return pl.pallas_call(
        add_kernel,
        in_specs=[VMEM, VMEM],
        out_specs=[VMEM] * 4,
        out_shape=[jax.ShapeDtypeStruct(shape, F32)] + [jax.ShapeDtypeStruct(shape, BF)] * 3,
        compiler_params=params(6),
        cost_estimate=cost(own.size, 9 * own.size),
        name="pair",
    )(own, theirs)


def prep_kernel(s, mine, other, after, hidden_t, a_out, b_out, mark):
    y = s[3]
    same = lax.rem(lax.rem(s[2] + s[4 + pl.program_id(0)], NZ), NC) == s[1]

    def turned(i):
        rows = [pl.ds(pl.multiple_of(lax.rem(y + j, NY) * TOK, TOK), TOK) for j in range(NY)]
        got = [jnp.where(same, mine[0, i, r, :], other[0, i, r, :]) for r in rows]
        return jnp.concatenate(got, axis=0).astype(F32)

    g, u = turned(0), turned(1)
    sig = 1.0 / (1.0 + jnp.exp(-g))
    gs = g * sig
    a_out[...] = gs
    b_out[...] = u * sig * (1.0 + g * (1.0 - sig))
    hidden_t[...] = (gs * u).astype(BF).T
    mark[...] = jnp.zeros(mark.shape, F32)


def prep(place, mine, other, after):
    ff = mine.shape[-1]
    tokens = NZ * BLK
    rows = pl.BlockSpec((BLK, ff), lambda t, s: (t, 0))

    def piece(t, s):
        block = lax.rem(s[2] + s[4 + t], NZ)
        return (lax.rem(lax.div(block, NC) - s[0] + NX, NX), 0, 0, 0)

    spec = pl.BlockSpec((1, 2, BLK, ff), piece)
    return pl.pallas_call(
        prep_kernel,
        grid_spec=pltpu.PrefetchScalarGridSpec(
            num_scalar_prefetch=1,
            grid=(NZ,),
            in_specs=[spec, spec, HBM],
            out_specs=[
                pl.BlockSpec((ff, BLK), lambda t, s: (0, t)),
                rows,
                rows,
                pl.BlockSpec((8, 128), lambda t, s: (0, 0)),
            ],
        ),
        out_shape=[
            jax.ShapeDtypeStruct((ff, tokens), BF),
            jax.ShapeDtypeStruct((tokens, ff), F32),
            jax.ShapeDtypeStruct((tokens, ff), F32),
            jax.ShapeDtypeStruct((8, 128), F32),
        ],
        compiler_params=params(8),
        cost_estimate=cost(30 * tokens * ff, 14 * tokens * ff),
        name="prep",
    )(place, mine, other, after)


def turn_kernel(s, x_in, after, x_out, mark):
    rows = [pl.ds(pl.multiple_of(lax.rem(s[3] + j, NY) * TOK, TOK), TOK) for j in range(NY)]
    x_out[...] = jnp.concatenate([x_in[r, :] for r in rows], axis=0).T
    mark[...] = jnp.zeros(mark.shape, F32)


def turn(place, x_all, after):
    tokens, width = x_all.shape
    return pl.pallas_call(
        turn_kernel,
        grid_spec=pltpu.PrefetchScalarGridSpec(
            num_scalar_prefetch=1,
            grid=(NZ,),
            in_specs=[pl.BlockSpec((BLK, width), lambda t, s: (lax.rem(s[2] + s[4 + t], NZ), 0)), HBM],
            out_specs=[
                pl.BlockSpec((width, BLK), lambda t, s: (0, t)),
                pl.BlockSpec((8, 128), lambda t, s: (0, 0)),
            ],
        ),
        out_shape=[jax.ShapeDtypeStruct((width, tokens), BF), jax.ShapeDtypeStruct((8, 128), F32)],
        compiler_params=params(8),
        cost_estimate=cost(0, 4 * tokens * width),
        name="turn",
    )(place, x_all, after)


def second_kernel(s, mine, other, a, b, gw, uw, after, dg, du, p):
    for j in range(dg.shape[0] // BLK):
        here = slice(j * SUB, (j + 1) * SUB)
        for half in range(NC):
            for xb in range(NX):
                k = lax.rem(xb - s[0] + NX, NX)
                d = jnp.where(s[1] == half, mine[k, here, :], other[k, here, :]).astype(F32)
                at = j * BLK + half * HALF + xb * SUB
                rows = slice(at, at + SUB)
                du[rows, :] = (d * a[rows, :]).astype(BF)
                dg[rows, :] = (d * b[rows, :]).astype(BF)
    p[...] = (nt(dg[...], gw[...]) + nt(du[...], uw[...])).astype(BF)


def second(place, mine, other, a, b, gate_weight, up_weight, at, n, after):
    ff = a.shape[1]
    width = gate_weight.shape[0]
    rows = n * BLK

    def whole(*shape):
        return pl.BlockSpec(shape, lambda t, s: (0,) * len(shape))

    got = pl.BlockSpec(
        (pl.Element(NX), pl.Element(n * SUB), pl.Element(ff)), lambda t, s: (0, at * SUB, 0)
    )
    row = pl.BlockSpec((pl.Element(rows), pl.Element(ff)), lambda t, s: (at * BLK, 0))
    return pl.pallas_call(
        second_kernel,
        grid_spec=pltpu.PrefetchScalarGridSpec(
            num_scalar_prefetch=1,
            grid=(1,),
            in_specs=[got, got, row, row, whole(width, ff), whole(width, ff), HBM],
            out_specs=[whole(rows, ff), whole(rows, ff), whole(rows, width)],
        ),
        out_shape=[
            pltpu.HBM((rows, ff), BF),
            pltpu.HBM((rows, ff), BF),
            jax.ShapeDtypeStruct((rows, width), BF),
        ],
        compiler_params=params(32),
        cost_estimate=cost(4 * rows * ff * width, 16 * rows * ff + 4 * ff * width),
        name="second",
    )(place, mine, other, a, b, gate_weight, up_weight, after)


def product_kernel(n, a, *refs):
    parts, (after, out, mark) = refs[:n], refs[n:]
    b = jnp.concatenate([v[...] for v in parts], axis=0)
    out[...] = jnp.dot(a[...], b, preferred_element_type=F32).astype(BF)
    mark[...] = jnp.zeros(mark.shape, F32)


def product(a, parts, tile, after):
    m, k = a.shape
    n = parts[0].shape[1]
    return pl.pallas_call(
        functools.partial(product_kernel, len(parts)),
        grid=(m // tile,),
        in_specs=[pl.BlockSpec((tile, k), lambda i: (i, 0))]
        + [pl.BlockSpec(v.shape, lambda i: (0, 0)) for v in parts]
        + [HBM],
        out_specs=[pl.BlockSpec((tile, n), lambda i: (i, 0)), pl.BlockSpec((8, 128), lambda i: (0, 0))],
        out_shape=[jax.ShapeDtypeStruct((m, n), BF), jax.ShapeDtypeStruct((8, 128), F32)],
        compiler_params=params(16),
        cost_estimate=cost(2 * m * k * n, 2 * (m * k + k * n + m * n)),
        name="product",
    )(a, *parts, after)


def near_kernel(bu, bd, up, down, *refs):
    up_out, down_out = refs[-2:]
    up_out[:HALF, :] = (bu[:HALF, :].astype(F32) + up[...].astype(F32)).astype(BF)
    up_out[HALF:, :] = bu[HALF:, :]
    down_out[:HALF, :] = bd[:HALF, :]
    down_out[HALF:, :] = (bd[HALF:, :].astype(F32) + down[...].astype(F32)).astype(BF)


def step_kernel(bu, bd, up, down, *refs):
    up_out, down_out = refs[-2:]
    up_out[...] = (bu[...].astype(F32) + up[...].astype(F32)).astype(BF)
    down_out[...] = (bd[...].astype(F32) + down[...].astype(F32)).astype(BF)


def step(kernel, p, i, j, up, down, *after):
    width = p.shape[1]
    sds = jax.ShapeDtypeStruct((BLK, width), BF)
    whole = pl.BlockSpec(up.shape, lambda t: (0, 0))
    block = pl.BlockSpec((BLK, width), lambda t: (0, 0))
    return pl.pallas_call(
        kernel,
        grid=(1,),
        in_specs=[
            pl.BlockSpec((BLK, width), lambda t: (i, 0)),
            pl.BlockSpec((BLK, width), lambda t: (j, 0)),
            whole,
            whole,
        ]
        + [HBM] * len(after),
        out_specs=[block, block],
        out_shape=[sds, sds],
        compiler_params=params(6),
        cost_estimate=cost(2 * BLK * width, 12 * BLK * width),
        name="step",
    )(p, p, up, down, *after)


def own_kernel(b0, up, down, after, own, s1, s2, s3):
    total = b0[...].astype(F32) + up[...].astype(F32) + down[...].astype(F32)
    own[...] = total[:TOK, :]
    for k, out in enumerate((s1, s2, s3), 1):
        out[...] = total[k * TOK:(k + 1) * TOK, :].astype(BF)


def own_of(p, up, down, after):
    width = p.shape[1]
    block = pl.BlockSpec((BLK, width), lambda t: (0, 0))
    out = pl.BlockSpec((TOK, width), lambda t: (0, 0))
    return pl.pallas_call(
        own_kernel,
        grid=(1,),
        in_specs=[block] * 3 + [HBM],
        out_specs=[out] * 4,
        out_shape=[jax.ShapeDtypeStruct((TOK, width), F32)] + [jax.ShapeDtypeStruct((TOK, width), BF)] * 3,
        compiler_params=params(6),
        cost_estimate=cost(2 * BLK * width, 8 * BLK * width),
        name="own",
    )(p, up, down, after)


def scatter_z_y(p, up, down, marks):
    for mark, i, j in ((marks[0], 2, 3), (marks[1], 1, 4)):
        up, down = step(step_kernel, p, i, j, from_z(up, -1), from_z(down, 1), mark)
    own, *sent = own_of(p, from_z(up, -1), from_z(down, 1), marks[2])
    return total_of(own, [from_y(v, -k) for k, v in enumerate(sent, 1)])


def on_device(
    inputs,
    cotangent,
    gate_pre,
    up_pre,
    gate_weight,
    up_weight,
    down_weight,
    pair_ids,
    flags,
    pair_scale,
):
    row, col = lax.axis_index("row"), lax.axis_index("col")
    place = jnp.stack([row // NC, row % NC, col // NY, col % NY] + [jnp.int32(t) for t in ORDER])
    place = place.astype(jnp.int32)
    scaled = weigh(cotangent, pair_ids, flags, pair_scale)
    x_all = lax.all_gather(inputs, "col", axis=0, tiled=True)

    dy0 = jnp.concatenate([scaled] + [from_y(scaled, k) for k in range(1, NY)], axis=0)
    pre = pack(gate_pre, up_pre, scaled)
    up, down = [dy0], [dy0]
    for _ in range(3):
        up.append(from_z(up[-1], 1))
        down.append(from_z(down[-1], -1))
    next_pre, last_pre = from_x(pre, 1), from_x(pre, -1)
    far_pre = from_x(next_pre[0], 1), from_x(last_pre[1], -1)
    low, high = halves(up[3], down[3], far_pre)
    low, high = from_z(low, 1), from_z(high, -1)
    dy = jnp.stack(up[:3] + [down[2], down[1], up[3], down[3]], axis=0)
    pre_mine = jnp.stack([pre, next_pre, jnp.stack(far_pre, axis=0), last_pre], axis=0)
    pre_other = from_core(pre_mine)

    sent = first(place, dy, low, high, down_weight, 1)
    hidden_t, a, b, ready = prep(place, pre_mine, pre_other, sent)
    own, *parts = pair_sums(first(place, dy, low, high, down_weight, 0), from_core(sent))
    total = total_of(own, [from_x(v, -k) for k, v in enumerate(parts, 1)], ready)
    flat = dy.reshape(-1, dy.shape[2])
    grad_down, mark_0 = product(hidden_t, [flat, low, high], 448, total)
    mine = join([total] + [from_x(total, k) for k in range(1, NX)], mark_0)
    args = place, mine, from_core(mine), a, b, gate_weight, up_weight
    far = second(*args, 7, 1, mark_0)
    last = far[2]
    ends = from_z(last[:HALF], -1), from_z(last[HALF:], 1)
    middle = second(*args, 5, 2, last)
    ends = step(near_kernel, middle[2], 0, 1, *ends)
    near = second(*args, 0, 5, ends[0])
    d_gate, d_up, _ = zip(near, middle, far)

    x_t, mark_1 = turn(place, x_all, near[2])
    grad_gate, mark_2 = product(x_t, d_gate, 512, mark_1)
    grad_up, mark_3 = product(x_t, d_up, 512, mark_2)
    grad_input = scatter_z_y(near[2], *ends, (mark_1, mark_2, mark_3))
    return (grad_input, grad_gate, grad_up, grad_down)


def solution(mesh):
    return jax.shard_map(
        on_device,
        mesh=mesh,
        in_specs=(
            P("col", "row"),
            P("col", "row"),
            P("row", "col"),
            P("row", "col"),
            P("row", "col"),
            P("row", "col"),
            P("col", "row"),
            P("col"),
            P("col"),
            P(),
        ),
        out_specs=(P("col", "row"), P("row", "col"), P("row", "col"), P("col", "row")),
        check_vma=False,
    )
```

```python
import functools

import jax
import jax.numpy as jnp
from jax import lax
from jax.experimental import pallas as pl
from jax.experimental.pallas import tpu as pltpu
from jax.sharding import PartitionSpec as P

NX, NC, NZ, NY = 4, 2, 8, 4
TOK = 32
BLK = NY * TOK
HALF = BLK // NC
SUB = HALF // NX
ORDER = (0, 1, 2, 6, 7, 3, 5, 4)
BF, F32 = jnp.bfloat16, jnp.float32
HBM = pl.BlockSpec(memory_space=pltpu.HBM)
VMEM = pl.BlockSpec(memory_space=pltpu.VMEM)
SMEM = pl.BlockSpec(memory_space=pltpu.SMEM)


def stay(v):
    return pltpu.with_memory_space_constraint(v, pltpu.HBM)


def params(mib):
    return pltpu.CompilerParams(vmem_limit_bytes=mib << 20)


def cost(flops, size):
    return pl.CostEstimate(flops=flops, bytes_accessed=size, transcendentals=0)


def from_z(v, k):
    perm = [(z * NY + y, (z - k) % NZ * NY + y) for z in range(NZ) for y in range(NY)]
    return lax.ppermute(v, "col", perm)


def from_y(v, k):
    perm = [(z * NY + y, z * NY + (y - k) % NY) for z in range(NZ) for y in range(NY)]
    return lax.ppermute(v, "col", perm)


def from_x(v, k):
    perm = [(x * NC + c, (x - k) % NX * NC + c) for x in range(NX) for c in range(NC)]
    return lax.ppermute(v, "row", perm)


def from_core(v):
    return lax.ppermute(v, "row", [(r, r ^ 1) for r in range(NX * NC)])


def weigh_kernel(ids_in, flags_in, scale_in, cot_in, out, ids, flags, scale, cot, sems):
    copies = [
        pltpu.make_async_copy(src, dst, sems.at[i])
        for i, (src, dst) in enumerate(
            ((ids_in, ids), (flags_in, flags), (scale_in, scale), (cot_in, cot))
        )
    ]
    for copy in copies:
        copy.start()
    for copy in copies:
        copy.wait()
    row = lax.broadcasted_iota(jnp.int32, cot.shape, 0)
    weight = jnp.zeros(cot.shape, F32)
    for r in range(TOK):
        w = (2 * flags[r] - 1).astype(F32) * scale[ids[r]]
        weight = jnp.where(row == r, w, weight)
    out[...] = (cot[...].astype(F32) * weight).astype(BF)


def weigh(cotangent, pair_ids, flags, pair_scale):
    return pl.pallas_call(
        weigh_kernel,
        in_specs=[HBM] * 4,
        out_specs=VMEM,
        out_shape=jax.ShapeDtypeStruct(cotangent.shape, BF),
        scratch_shapes=[
            pltpu.SMEM(pair_ids.shape, jnp.int32),
            pltpu.SMEM(flags.shape, jnp.int32),
            pltpu.SMEM(pair_scale.shape, F32),
            pltpu.VMEM(cotangent.shape, BF),
            pltpu.SemaphoreType.DMA((4,)),
        ],
        compiler_params=params(4),
        cost_estimate=cost(cotangent.size, 8 * cotangent.size),
        name="weigh",
    )(*map(stay, (pair_ids, flags, pair_scale, cotangent)))


def pack_kernel(g, u, after, pre, sems):
    copies = [pltpu.make_async_copy(v, pre.at[i], sems.at[i]) for i, v in enumerate((g, u))]
    for copy in copies:
        copy.start()
    for copy in copies:
        copy.wait()


def pack(gate_pre, up_pre, after):
    return pl.pallas_call(
        pack_kernel,
        in_specs=[HBM] * 3,
        out_specs=VMEM,
        out_shape=jax.ShapeDtypeStruct((2,) + gate_pre.shape, BF),
        scratch_shapes=[pltpu.SemaphoreType.DMA((2,))],
        compiler_params=params(4),
        cost_estimate=cost(0, 8 * gate_pre.size),
        name="pack",
    )(stay(gate_pre), stay(up_pre), after)


def halves_kernel(u, d, r1, r2, low, high):
    low[...] = u[:HALF, :]
    high[...] = d[HALF:, :]


def halves(u, d, after):
    half = jax.ShapeDtypeStruct((HALF, u.shape[1]), BF)
    return pl.pallas_call(
        halves_kernel,
        in_specs=[VMEM] * 2 + [HBM] * 2,
        out_specs=[VMEM] * 2,
        out_shape=[half, half],
        compiler_params=params(4),
        cost_estimate=cost(0, 4 * u.size),
        name="halves",
    )(u, d, *after)


def nt(a, b):
    return lax.dot_general(a, b, (((1,), (1,)), ((), ())), preferred_element_type=F32)


def first_kernel(flip, s, dy, low, high, w, out):
    n = dy.shape[0]
    far = jnp.where(lax.rem(s[1] + flip, NC) == 0, low[...], high[...])
    rows = jnp.concatenate([dy[j] for j in range(n)] + [far], axis=0)
    acc = nt(rows, w[...]).astype(out.dtype)
    for xb in range(NX):
        k = lax.rem(xb - s[0] + NX, NX)
        for j in range(n + 1):
            at = j * HALF + xb * SUB
            out[k, j * SUB:(j + 1) * SUB, :] = acc[at:at + SUB, :]


def first(place, dy, low, high, w, flip):
    ff, width = w.shape
    n = dy.shape[0]
    rows = NZ * SUB
    far = pl.BlockSpec((HALF, width), lambda i, s: (0, 0))
    return pl.pallas_call(
        functools.partial(first_kernel, flip),
        grid_spec=pltpu.PrefetchScalarGridSpec(
            num_scalar_prefetch=1,
            grid=(1,),
            in_specs=[
                pl.BlockSpec((n, HALF, width), lambda i, s: (0, lax.rem(s[1] + flip, NC), 0)),
                far,
                far,
                pl.BlockSpec((ff, width), lambda i, s: (0, 0)),
            ],
            out_specs=pl.BlockSpec((NX, rows, ff), lambda i, s: (0, 0, 0)),
        ),
        out_shape=jax.ShapeDtypeStruct((NX, rows, ff), BF if flip else F32),
        compiler_params=params(16),
        cost_estimate=cost(2 * NX * rows * ff * width, 2 * ff * width + 4 * NX * rows * (ff + width)),
        name="first",
    )(place, dy, low, high, w)


def total_kernel(own, r1, r2, r3, *refs):
    refs[-1][...] = (own[...] + r1[...].astype(F32) + r2[...].astype(F32) + r3[...].astype(F32)).astype(BF)


def total_of(own, parts, *after):
    return pl.pallas_call(
        total_kernel,
        in_specs=[VMEM] * 4 + [HBM] * len(after),
        out_specs=VMEM,
        out_shape=jax.ShapeDtypeStruct(own.shape, BF),
        compiler_params=params(4),
        cost_estimate=cost(3 * own.size, 12 * own.size),
        name="total",
    )(own, *parts, *after)


def join_kernel(a, b, c, d, after, out):
    for k, v in enumerate((a, b, c, d)):
        out[k] = v[...]


def join(parts, after):
    shape = parts[0].shape
    return pl.pallas_call(
        join_kernel,
        in_specs=[VMEM] * 4 + [HBM],
        out_specs=VMEM,
        out_shape=jax.ShapeDtypeStruct((NX,) + shape, BF),
        compiler_params=params(4),
        cost_estimate=cost(0, 16 * parts[0].size),
        name="join",
    )(*parts, after)


def add_kernel(own, theirs, mine, s1, s2, s3):
    mine[...] = own[0] + theirs[0].astype(F32)
    for k, out in enumerate((s1, s2, s3), 1):
        out[...] = (own[k] + theirs[k].astype(F32)).astype(BF)


def pair_sums(own, theirs):
    shape = own.shape[1:]
    return pl.pallas_call(
        add_kernel,
        in_specs=[VMEM, VMEM],
        out_specs=[VMEM] * 4,
        out_shape=[jax.ShapeDtypeStruct(shape, F32)] + [jax.ShapeDtypeStruct(shape, BF)] * 3,
        compiler_params=params(6),
        cost_estimate=cost(own.size, 9 * own.size),
        name="pair",
    )(own, theirs)


def prep_kernel(s, mine, other, after, hidden_t, a_out, b_out, mark):
    y = s[3]
    same = lax.rem(lax.rem(s[2] + s[4 + pl.program_id(0)], NZ), NC) == s[1]

    def turned(i):
        rows = [pl.ds(pl.multiple_of(lax.rem(y + j, NY) * TOK, TOK), TOK) for j in range(NY)]
        got = [jnp.where(same, mine[0, i, r, :], other[0, i, r, :]) for r in rows]
        return jnp.concatenate(got, axis=0).astype(F32)

    g, u = turned(0), turned(1)
    sig = 1.0 / (1.0 + jnp.exp(-g))
    gs = g * sig
    a_out[...] = gs
    b_out[...] = u * sig * (1.0 + g * (1.0 - sig))
    hidden_t[...] = (gs * u).astype(BF).T
    mark[...] = jnp.zeros(mark.shape, F32)


def prep(place, mine, other, after):
    ff = mine.shape[-1]
    tokens = NZ * BLK
    rows = pl.BlockSpec((BLK, ff), lambda t, s: (t, 0))

    def piece(t, s):
        block = lax.rem(s[2] + s[4 + t], NZ)
        return (lax.rem(lax.div(block, NC) - s[0] + NX, NX), 0, 0, 0)

    spec = pl.BlockSpec((1, 2, BLK, ff), piece)
    return pl.pallas_call(
        prep_kernel,
        grid_spec=pltpu.PrefetchScalarGridSpec(
            num_scalar_prefetch=1,
            grid=(NZ,),
            in_specs=[spec, spec, HBM],
            out_specs=[
                pl.BlockSpec((ff, BLK), lambda t, s: (0, t)),
                rows,
                rows,
                pl.BlockSpec((8, 128), lambda t, s: (0, 0)),
            ],
        ),
        out_shape=[
            jax.ShapeDtypeStruct((ff, tokens), BF),
            jax.ShapeDtypeStruct((tokens, ff), F32),
            jax.ShapeDtypeStruct((tokens, ff), F32),
            jax.ShapeDtypeStruct((8, 128), F32),
        ],
        compiler_params=params(8),
        cost_estimate=cost(30 * tokens * ff, 14 * tokens * ff),
        name="prep",
    )(place, mine, other, after)


def turn_kernel(s, x_in, after, x_out, mark):
    rows = [pl.ds(pl.multiple_of(lax.rem(s[3] + j, NY) * TOK, TOK), TOK) for j in range(NY)]
    x_out[...] = jnp.concatenate([x_in[r, :] for r in rows], axis=0).T
    mark[...] = jnp.zeros(mark.shape, F32)


def turn(place, x_all, after):
    tokens, width = x_all.shape
    return pl.pallas_call(
        turn_kernel,
        grid_spec=pltpu.PrefetchScalarGridSpec(
            num_scalar_prefetch=1,
            grid=(NZ,),
            in_specs=[pl.BlockSpec((BLK, width), lambda t, s: (lax.rem(s[2] + s[4 + t], NZ), 0)), HBM],
            out_specs=[
                pl.BlockSpec((width, BLK), lambda t, s: (0, t)),
                pl.BlockSpec((8, 128), lambda t, s: (0, 0)),
            ],
        ),
        out_shape=[jax.ShapeDtypeStruct((width, tokens), BF), jax.ShapeDtypeStruct((8, 128), F32)],
        compiler_params=params(8),
        cost_estimate=cost(0, 4 * tokens * width),
        name="turn",
    )(place, x_all, after)


def second_kernel(s, mine, other, a, b, gw, uw, after, dg, du, p):
    for j in range(dg.shape[0] // BLK):
        here = slice(j * SUB, (j + 1) * SUB)
        for half in range(NC):
            for xb in range(NX):
                k = lax.rem(xb - s[0] + NX, NX)
                d = jnp.where(s[1] == half, mine[k, here, :], other[k, here, :]).astype(F32)
                at = j * BLK + half * HALF + xb * SUB
                rows = slice(at, at + SUB)
                du[rows, :] = (d * a[rows, :]).astype(BF)
                dg[rows, :] = (d * b[rows, :]).astype(BF)
    p[...] = (nt(dg[...], gw[...]) + nt(du[...], uw[...])).astype(BF)


def second(place, mine, other, a, b, gate_weight, up_weight, at, n, after):
    ff = a.shape[1]
    width = gate_weight.shape[0]
    rows = n * BLK

    def whole(*shape):
        return pl.BlockSpec(shape, lambda t, s: (0,) * len(shape))

    got = pl.BlockSpec(
        (pl.Element(NX), pl.Element(n * SUB), pl.Element(ff)), lambda t, s: (0, at * SUB, 0)
    )
    row = pl.BlockSpec((pl.Element(rows), pl.Element(ff)), lambda t, s: (at * BLK, 0))
    return pl.pallas_call(
        second_kernel,
        grid_spec=pltpu.PrefetchScalarGridSpec(
            num_scalar_prefetch=1,
            grid=(1,),
            in_specs=[got, got, row, row, whole(width, ff), whole(width, ff), HBM],
            out_specs=[whole(rows, ff), whole(rows, ff), whole(rows, width)],
        ),
        out_shape=[
            pltpu.HBM((rows, ff), BF),
            pltpu.HBM((rows, ff), BF),
            jax.ShapeDtypeStruct((rows, width), BF),
        ],
        compiler_params=params(32),
        cost_estimate=cost(4 * rows * ff * width, 16 * rows * ff + 4 * ff * width),
        name="second",
    )(place, mine, other, a, b, gate_weight, up_weight, after)


def product_kernel(n, a, *refs):
    parts, (after, out, mark) = refs[:n], refs[n:]
    b = jnp.concatenate([v[...] for v in parts], axis=0)
    out[...] = jnp.dot(a[...], b, preferred_element_type=F32).astype(BF)
    mark[...] = jnp.zeros(mark.shape, F32)


def product(a, parts, tile, after):
    m, k = a.shape
    n = parts[0].shape[1]
    return pl.pallas_call(
        functools.partial(product_kernel, len(parts)),
        grid=(m // tile,),
        in_specs=[pl.BlockSpec((tile, k), lambda i: (i, 0))]
        + [pl.BlockSpec(v.shape, lambda i: (0, 0)) for v in parts]
        + [HBM],
        out_specs=[pl.BlockSpec((tile, n), lambda i: (i, 0)), pl.BlockSpec((8, 128), lambda i: (0, 0))],
        out_shape=[jax.ShapeDtypeStruct((m, n), BF), jax.ShapeDtypeStruct((8, 128), F32)],
        compiler_params=params(16),
        cost_estimate=cost(2 * m * k * n, 2 * (m * k + k * n + m * n)),
        name="product",
    )(a, *parts, after)


def near_kernel(bu, bd, up, down, *refs):
    up_out, down_out = refs[-2:]
    up_out[:HALF, :] = (bu[:HALF, :].astype(F32) + up[...].astype(F32)).astype(BF)
    up_out[HALF:, :] = bu[HALF:, :]
    down_out[:HALF, :] = bd[:HALF, :]
    down_out[HALF:, :] = (bd[HALF:, :].astype(F32) + down[...].astype(F32)).astype(BF)


def step_kernel(bu, bd, up, down, *refs):
    up_out, down_out = refs[-2:]
    up_out[...] = (bu[...].astype(F32) + up[...].astype(F32)).astype(BF)
    down_out[...] = (bd[...].astype(F32) + down[...].astype(F32)).astype(BF)


def step(kernel, p, i, j, up, down, *after):
    width = p.shape[1]
    sds = jax.ShapeDtypeStruct((BLK, width), BF)
    whole = pl.BlockSpec(up.shape, lambda t: (0, 0))
    block = pl.BlockSpec((BLK, width), lambda t: (0, 0))
    return pl.pallas_call(
        kernel,
        grid=(1,),
        in_specs=[
            pl.BlockSpec((BLK, width), lambda t: (i, 0)),
            pl.BlockSpec((BLK, width), lambda t: (j, 0)),
            whole,
            whole,
        ]
        + [HBM] * len(after),
        out_specs=[block, block],
        out_shape=[sds, sds],
        compiler_params=params(6),
        cost_estimate=cost(2 * BLK * width, 12 * BLK * width),
        name="step",
    )(p, p, up, down, *after)


def own_kernel(b0, up, down, after, own, s1, s2, s3):
    total = b0[...].astype(F32) + up[...].astype(F32) + down[...].astype(F32)
    own[...] = total[:TOK, :]
    for k, out in enumerate((s1, s2, s3), 1):
        out[...] = total[k * TOK:(k + 1) * TOK, :].astype(BF)


def own_of(p, up, down, after):
    width = p.shape[1]
    block = pl.BlockSpec((BLK, width), lambda t: (0, 0))
    out = pl.BlockSpec((TOK, width), lambda t: (0, 0))
    return pl.pallas_call(
        own_kernel,
        grid=(1,),
        in_specs=[block] * 3 + [HBM],
        out_specs=[out] * 4,
        out_shape=[jax.ShapeDtypeStruct((TOK, width), F32)] + [jax.ShapeDtypeStruct((TOK, width), BF)] * 3,
        compiler_params=params(6),
        cost_estimate=cost(2 * BLK * width, 8 * BLK * width),
        name="own",
    )(p, up, down, after)


def on_device(
    inputs,
    cotangent,
    gate_pre,
    up_pre,
    gate_weight,
    up_weight,
    down_weight,
    pair_ids,
    flags,
    pair_scale,
):
    row, col = lax.axis_index("row"), lax.axis_index("col")
    place = jnp.stack([row // NC, row % NC, col // NY, col % NY] + [jnp.int32(t) for t in ORDER])
    place = place.astype(jnp.int32)
    scaled = weigh(cotangent, pair_ids, flags, pair_scale)
    x_all = lax.all_gather(inputs, "col", axis=0, tiled=True)

    dy0 = jnp.concatenate([scaled] + [from_y(scaled, k) for k in range(1, NY)], axis=0)
    pre = pack(gate_pre, up_pre, scaled)
    up, down = [dy0], [dy0]
    for _ in range(3):
        up.append(from_z(up[-1], 1))
        down.append(from_z(down[-1], -1))
    next_pre, last_pre = from_x(pre, 1), from_x(pre, -1)
    far_pre = from_x(next_pre[0], 1), from_x(last_pre[1], -1)
    low, high = halves(up[3], down[3], far_pre)
    low, high = from_z(low, 1), from_z(high, -1)
    dy = jnp.stack(up[:3] + [down[2], down[1], up[3], down[3]], axis=0)
    pre_mine = jnp.stack([pre, next_pre, jnp.stack(far_pre, axis=0), last_pre], axis=0)
    pre_other = from_core(pre_mine)

    sent = first(place, dy, low, high, down_weight, 1)
    hidden_t, a, b, ready = prep(place, pre_mine, pre_other, sent)
    own, *parts = pair_sums(first(place, dy, low, high, down_weight, 0), from_core(sent))
    total = total_of(own, [from_x(v, -k) for k, v in enumerate(parts, 1)], ready)
    flat = dy.reshape(-1, dy.shape[2])
    grad_down, mark_0 = product(hidden_t, [flat, low, high], 448, total)
    mine = join([total] + [from_x(total, k) for k in range(1, NX)], mark_0)
    args = place, mine, from_core(mine), a, b, gate_weight, up_weight
    far = second(*args, 7, 1, mark_0)
    last = far[2]
    ends = from_z(last[:HALF], -1), from_z(last[HALF:], 1)
    middle = second(*args, 5, 2, last)
    ends = step(near_kernel, middle[2], 0, 1, *ends)
    near = second(*args, 0, 5, ends[0])
    d_gate, d_up, _ = zip(near, middle, far)

    ends = step(step_kernel, near[2], 2, 3, from_z(ends[0], -1), from_z(ends[1], 1))
    x_t, mark = turn(place, x_all, ends[0])
    ends = step(step_kernel, near[2], 1, 4, from_z(ends[0], -1), from_z(ends[1], 1), mark)
    grad_gate, mark = product(x_t, d_gate, 512, ends[0])
    own, *sent = own_of(near[2], from_z(ends[0], -1), from_z(ends[1], 1), mark)
    grad_up, mark = product(x_t, d_up, 512, sent[0])
    grad_input = total_of(own, [from_y(v, -k) for k, v in enumerate(sent, 1)], mark)
    return (grad_input, grad_gate, grad_up, grad_down)


def solution(mesh):
    return jax.shard_map(
        on_device,
        mesh=mesh,
        in_specs=(
            P("col", "row"),
            P("col", "row"),
            P("row", "col"),
            P("row", "col"),
            P("row", "col"),
            P("row", "col"),
            P("col", "row"),
            P("col"),
            P("col"),
            P(),
        ),
        out_specs=(P("col", "row"), P("row", "col"), P("row", "col"), P("col", "row")),
        check_vma=False,
    )
```
